32 devices in a mesh: space: 4 (over x, core), energy: 8 (over z, y).
Axes of the slice: x: 2, y: 2, z: 4, core: 2. Of those that a mesh axis runs over, the one named last changes fastest.
Arguments:
- green_lower: bfloat16 [4, 32, 2, 128, 128], P('space', 'energy'), may hold values from -0.5 to 0.5
- green_diag: bfloat16 [4, 32, 2, 128, 128], P('space', 'energy'), may hold values from -0.5 to 0.5
- green_upper: bfloat16 [4, 32, 2, 128, 128], P('space', 'energy'), may hold values from -0.5 to 0.5
- self_energy: bfloat16 [2, 4, 32, 2, 128, 128], P(None, 'space', 'energy'), may hold values from -1.75 to 1.75
- coulomb: bfloat16 [4, 128, 128], P('space'), may hold values from -0.5 to 0.5
Outputs:
- screened_polarization: bfloat16 [2, 4, 32, 2, 128, 128], P(None, 'space', 'energy')
The draws below stay inside these ranges and needn't reach their ends.
All inputs are finite; a program needn't handle non-finite values.
Results may differ from the reference program's by a relative error of at most 0.017.
Values may be sent and summed in bfloat16 or wider, within the bound.
A program may use at most 64 MiB of HBM per device.

```python
import jax
import jax.numpy as jnp
from jax import lax

B = 128
NBLOCKS = 4
ENERGIES = 32
PADDED = 64


def shard_levels(stream_key, shape, shards, low, largest):
    factor_of = 1.0
    for dim, parts in shards:
        heights = jax.random.uniform(jax.random.fold_in(jax.random.fold_in(stream_key, 6), dim), (parts,), jnp.float32, low / len(shards), largest / len(shards))
        factor_of = factor_of * jnp.repeat(jnp.exp(heights), shape[dim] // parts).reshape((-1,) + (1,) * (len(shape) - 1 - dim))
    return factor_of


def noise(own_key, shape, width, bound, cuts=(), held_as=jnp.bfloat16):
    gain = shard_levels(own_key, shape, cuts, -0.22, 0.18) if cuts else 1.0
    values = jax.random.normal(own_key, shape, jnp.float32) * width * gain
    return jnp.minimum(jnp.maximum(values, -bound), bound).astype(held_as)


def setup_inputs(seed: int = 0) -> dict:
    arg_keys = jax.random.split(jax.random.key(seed), 6)
    green_lower = noise(arg_keys[0], (NBLOCKS, ENERGIES, 2, B, B), B ** -0.5, 0.5, ((0, 4), (1, 8)))
    green_diag = noise(arg_keys[1], (NBLOCKS, ENERGIES, 2, B, B), B ** -0.5, 0.5, ((0, 4), (1, 8)))
    green_upper = noise(arg_keys[2], (NBLOCKS, ENERGIES, 2, B, B), B ** -0.5, 0.5, ((0, 4), (1, 8)))
    self_energy = noise(arg_keys[3], (2, NBLOCKS, ENERGIES, 2, B, B), 0.3, 1.75, ((1, 4), (2, 8)))
    coulomb = noise(arg_keys[4], (NBLOCKS, B, B), B ** -0.5, 0.5, ((0, 4),))
    return {"green_lower": green_lower, "green_diag": green_diag, "green_upper": green_upper, "self_energy": self_energy, "coulomb": coulomb}


def to_bfloat(values):
    return lax.optimization_barrier(values.astype(jnp.bfloat16)).astype(jnp.float32)


def congruence(green, sigma):
    green = green.astype(jnp.float32)
    sigma = sigma.astype(jnp.float32)
    green_real = green[:, 0]
    green_imag = green[:, 1]
    sigma_real = sigma[:, :, 0]
    sigma_imag = sigma[:, :, 1]
    mixed_real = to_bfloat(jnp.einsum('epq,feqr->fepr', green_real, sigma_real) - jnp.einsum('epq,feqr->fepr', green_imag, sigma_imag))
    mixed_imag = to_bfloat(jnp.einsum('epq,feqr->fepr', green_real, sigma_imag) + jnp.einsum('epq,feqr->fepr', green_imag, sigma_real))
    result_real = jnp.einsum('fepr,esr->feps', mixed_real, green_real) + jnp.einsum('fepr,esr->feps', mixed_imag, green_imag)
    result_imag = jnp.einsum('fepr,esr->feps', mixed_imag, green_real) - jnp.einsum('fepr,esr->feps', mixed_real, green_imag)
    return result_real, result_imag


def reference(green_lower, green_diag, green_upper, self_energy, coulomb):
    sigma_padded = jnp.pad(self_energy, ((0, 0), (1, 1), (0, 0), (0, 0), (0, 0), (0, 0)))
    factor = ENERGIES ** -0.5

    def one_block(block_id):
        lower_green = lax.dynamic_index_in_dim(green_lower, block_id, 0, keepdims=False)
        diag_green = lax.dynamic_index_in_dim(green_diag, block_id, 0, keepdims=False)
        upper_green = lax.dynamic_index_in_dim(green_upper, block_id, 0, keepdims=False)
        window = lax.dynamic_slice_in_dim(sigma_padded, block_id, 3, 1)
        first = congruence(lower_green, window[:, 0])
        second = congruence(diag_green, window[:, 1])
        third = congruence(upper_green, window[:, 2])
        total_real = first[0] + second[0] + third[0]
        total_imag = first[1] + second[1] + third[1]
        green_function = to_bfloat(jnp.stack([total_real, total_imag], axis=2))
        complex_values = lax.complex(green_function[:, :, 0], green_function[:, :, 1])
        spectra = jnp.fft.fft(complex_values, n=PADDED, axis=1)
        correlation = jnp.fft.ifft(spectra[0] * jnp.conj(spectra[1]), axis=0)
        lag_index = jnp.arange(ENERGIES)
        lesser = correlation[:ENERGIES] * factor
        greater = jnp.conj(correlation[(PADDED - lag_index) % PADDED]) * factor
        polar = to_bfloat(jnp.stack([jnp.stack([jnp.real(lesser), jnp.imag(lesser)], axis=1), jnp.stack([jnp.real(greater), jnp.imag(greater)], axis=1)], axis=0))
        coulomb_block = lax.dynamic_index_in_dim(coulomb, block_id, 0, keepdims=False).astype(jnp.float32)
        left_product = to_bfloat(jnp.einsum('pq,fetqr->fetpr', coulomb_block, polar))
        return jnp.einsum('fetpr,sr->fetps', left_product, coulomb_block).astype(jnp.bfloat16)

    stacked = lax.map(one_block, jnp.arange(NBLOCKS, dtype=jnp.int32))
    return jnp.moveaxis(stacked, 0, 1)
```

```python
import functools
import math

import jax
import jax.numpy as jnp
from jax import lax
from jax.experimental import pallas as pl
from jax.experimental.pallas import tpu as pltpu
from jax.sharding import PartitionSpec as P


def padded_2(shard, sides, width):
    for axis, dim in sides:
        peers, length = (lax.axis_size(axis), shard.shape[dim])
        up = [(i, (i + 1) % peers) for i in range(peers - 1)]
        down = [(j, i) for i, j in up]
        last = lax.slice_in_dim(shard, length - width, length, axis=dim)
        initial = lax.slice_in_dim(shard, 0, width, axis=dim)
        before = lax.ppermute(last, axis, up)
        after = lax.ppermute(initial, axis, down)
        shard = jnp.concatenate([before, shard, after], axis=dim)
    return shard


def congruence(green, sigma):
    green_real = green[:, :, 0]
    green_imag = green[:, :, 1]
    sigma_real = sigma[:, :, :, 0]
    sigma_imag = sigma[:, :, :, 1]
    green_wide = jnp.concatenate([green_real, green_imag], axis=-1)
    sigma_tall = jnp.concatenate(
        [
            jnp.concatenate([sigma_real, sigma_imag], axis=-1),
            jnp.concatenate([-sigma_imag, sigma_real], axis=-1),
        ],
        axis=-2,
    )
    mixed = jnp.einsum(
        "nepq,fneqr->fnepr", green_wide, sigma_tall, preferred_element_type=jnp.float32
    ).astype(jnp.bfloat16)
    adjoint_tall = jnp.concatenate(
        [green_wide, jnp.concatenate([-green_imag, green_real], axis=-1)], axis=-2
    )
    return jnp.einsum("fnepr,nesr->fneps", mixed, adjoint_tall, preferred_element_type=jnp.float32)


def split_table(table):
    high_part = table.astype(jnp.bfloat16)
    low_part = (table - high_part.astype(jnp.float32)).astype(jnp.bfloat16)
    return (high_part, low_part)


def spectrum(values, table_high, table_low, padded_len):

    def apply_table(part):
        return jnp.dot(table_high, part, preferred_element_type=jnp.float32) + jnp.dot(
            table_low, part, preferred_element_type=jnp.float32
        )

    real_terms = apply_table(values[:, 0])
    imag_terms = apply_table(values[:, 1])
    out_real = real_terms[:padded_len] + imag_terms[padded_len:]
    out_imag = imag_terms[:padded_len] - real_terms[padded_len:]
    return (out_real, out_imag)


def plain_body(green_lower, green_diag, green_upper, self_energy, coulomb):
    block_count = green_diag.shape[0]
    energy_local = green_diag.shape[1]
    block_order = green_diag.shape[-1]
    energies = energy_local * lax.axis_size("energy")
    padded_len = 2 * energies
    padded = padded_2(self_energy, (("space", 1),), 1)
    lower_term = congruence(green_lower, padded[:, :block_count])
    diag_term = congruence(green_diag, padded[:, 1 : block_count + 1])
    upper_term = congruence(green_upper, padded[:, 2:])
    total = lower_term + diag_term + upper_term
    total = total.reshape(2, block_count, energy_local, block_order, 2, block_order)
    green_function = (
        jnp.transpose(total, (0, 2, 4, 1, 3, 5))
        .astype(jnp.bfloat16)
        .reshape(2, energy_local, 2, -1)
    )
    frequency = lax.iota(jnp.int32, padded_len)
    energy_index = lax.iota(jnp.int32, energies)
    step_angle = 2.0 * math.pi / padded_len
    forward_angle = (frequency[:, None] * energy_index[None, :] % padded_len).astype(
        jnp.float32
    ) * step_angle
    forward_table = jnp.concatenate([jnp.cos(forward_angle), jnp.sin(forward_angle)], axis=0)
    table_high, table_low = split_table(forward_table)
    lesser_values = lax.all_to_all(
        green_function[0], "energy", split_axis=2, concat_axis=0, tiled=True
    )
    greater_values = lax.all_to_all(
        green_function[1], "energy", split_axis=2, concat_axis=0, tiled=True
    )
    lesser_real, lesser_imag = spectrum(lesser_values, table_high, table_low, padded_len)
    greater_real, greater_imag = spectrum(greater_values, table_high, table_low, padded_len)
    product_real = lesser_real * greater_real + lesser_imag * greater_imag
    product_imag = lesser_imag * greater_real - lesser_real * greater_imag
    row_index = jnp.concatenate([energy_index, (padded_len - energy_index) % padded_len])
    back_angle = (row_index[:, None] * frequency[None, :] % padded_len).astype(
        jnp.float32
    ) * step_angle
    back_cos = jnp.cos(back_angle)
    back_sin = jnp.sin(back_angle)
    back_table = jnp.concatenate(
        [
            jnp.concatenate([back_cos, -back_sin], axis=1),
            jnp.concatenate([back_sin, back_cos], axis=1),
        ],
        axis=0,
    )
    stacked_product = jnp.concatenate([product_real, product_imag], axis=0)
    factor = 1.0 / (padded_len * math.sqrt(energies))
    combined = (
        jnp.dot(
            back_table,
            stacked_product,
            precision=lax.Precision.HIGH,
            preferred_element_type=jnp.float32,
        )
        * factor
    )
    corr_real = combined[:padded_len]
    corr_imag = combined[padded_len:]
    lesser_lags = jnp.stack([corr_real[:energies], corr_imag[:energies]], axis=1)
    greater_lags = jnp.stack([corr_real[energies:], -corr_imag[energies:]], axis=1)
    polar = jnp.stack([lesser_lags, greater_lags], axis=0).astype(jnp.bfloat16)
    returned = lax.all_to_all(polar, "energy", split_axis=1, concat_axis=3, tiled=True)
    returned = returned.reshape(2, energy_local, 2, block_count, block_order, block_order)
    left_product = jnp.einsum(
        "npq,fetnqr->fetnpr", coulomb, returned, preferred_element_type=jnp.float32
    ).astype(jnp.bfloat16)
    screened = jnp.einsum(
        "fetnpr,nsr->fnetps", left_product, coulomb, preferred_element_type=jnp.float32
    )
    return screened.astype(jnp.bfloat16)


ROWS = 16
MESH = pl.DeviceIdType.MESH


def partner(me, step):
    other, bit = me, 1
    while bit <= step:
        if step & bit:
            other = other + bit * (1 - 2 * lax.rem(lax.div(me, bit), 2))
        bit *= 2
    return other


def far_first(peers):
    steps, span = [], peers // 2
    while span >= 1:
        steps += list(range(span, 2 * span))
        span //= 2
    return steps


def rotation(real, imag):
    return jnp.concatenate(
        [
            jnp.concatenate([real, imag], axis=1),
            jnp.concatenate([-imag, real], axis=1),
        ],
        axis=0,
    )


def fused_kernel(
    peers,
    sites,
    lower_ref,
    diag_ref,
    upper_ref,
    sigma_ref,
    coulomb_ref,
    out_ref,
    halo,
    green_out,
    green_in,
    series,
    polar_out,
    polar_in,
    halo_send,
    halo_recv,
    green_send,
    green_recv,
    polar_send,
    polar_recv,
):
    me = lax.axis_index("energy")
    site = lax.axis_index("space")
    has_next = site < sites - 1
    has_previous = site > 0
    next_site = lax.rem(site + 1, sites)
    previous_site = lax.rem(site + sites - 1, sites)
    local = diag_ref.shape[1]
    order = diag_ref.shape[-1]
    energies = peers * local
    steps = far_first(peers)
    f32 = jnp.float32

    barrier = pltpu.get_barrier_semaphore()
    for step in steps:
        pl.semaphore_signal(
            barrier, inc=1, device_id={"energy": partner(me, step)}, device_id_type=MESH
        )

    @pl.when(has_next)
    def _():
        pl.semaphore_signal(barrier, inc=1, device_id={"space": next_site}, device_id_type=MESH)

    @pl.when(has_previous)
    def _():
        pl.semaphore_signal(barrier, inc=1, device_id={"space": previous_site}, device_id_type=MESH)

    neighbours = jnp.where(has_next, 1, 0) + jnp.where(has_previous, 1, 0)
    pl.semaphore_wait(barrier, peers - 1 + neighbours)

    def halo_copy(side, energy):
        return pltpu.make_async_remote_copy(
            src_ref=sigma_ref.at[:, 0, energy],
            dst_ref=halo.at[side, energy],
            send_sem=halo_send.at[side, energy],
            recv_sem=halo_recv.at[side, energy],
            device_id={"space": next_site if side == 0 else previous_site},
            device_id_type=MESH,
        )

    for energy in range(local):

        @pl.when(has_next)
        def _():
            halo_copy(0, energy).start()

        @pl.when(has_previous)
        def _():
            halo_copy(1, energy).start()

    @pl.when(jnp.logical_not(has_previous))
    def _():
        halo[0] = jnp.zeros(halo.shape[1:], halo.dtype)

    @pl.when(jnp.logical_not(has_next))
    def _():
        halo[1] = jnp.zeros(halo.shape[1:], halo.dtype)

    def green_copy(other, slot, energy):
        return pltpu.make_async_remote_copy(
            src_ref=green_out.at[other, energy],
            dst_ref=green_in.at[slot, energy],
            send_sem=green_send.at[other, energy],
            recv_sem=green_recv.at[slot, energy],
            device_id={"energy": other},
            device_id_type=MESH,
        )

    def one_energy(energy, carry):
        def term(green_ref, sigma_of):
            real, imag = green_ref[0, energy, 0], green_ref[0, energy, 1]
            wide = jnp.concatenate([real, imag], axis=1)
            mixed = [
                jnp.dot(
                    wide,
                    rotation(sigma_of(kind, 0), sigma_of(kind, 1)),
                    preferred_element_type=f32,
                ).astype(jnp.bfloat16)
                for kind in range(2)
            ]
            return lax.dot_general(
                jnp.concatenate(mixed, axis=0),
                rotation(real, imag),
                (((1,), (1,)), ((), ())),
                preferred_element_type=f32,
            )

        total = term(diag_ref, lambda kind, part: sigma_ref[kind, 0, energy, part])

        @pl.when(has_previous)
        def _():
            halo_copy(0, energy).wait_recv()

        @pl.when(has_next)
        def _():
            halo_copy(1, energy).wait_recv()

        total += term(lower_ref, lambda kind, part: halo[0, energy, kind, part])
        total += term(upper_ref, lambda kind, part: halo[1, energy, kind, part])
        rounded = total.astype(jnp.bfloat16)
        for kind in range(2):
            for part in range(2):
                block = rounded[
                    kind * order : (kind + 1) * order, part * order : (part + 1) * order
                ]
                green_out[:, energy, kind, part] = block.reshape(peers, ROWS, order)
        for step in steps:
            green_copy(partner(me, step), me, energy).start()
        return carry

    lax.fori_loop(0, local, one_energy, 0)

    tail = series.shape[2] - energies
    for kind in range(2):
        for part in range(2):
            series[kind, part, energies:] = jnp.zeros((tail, ROWS, order), f32)

    def unpack(source, values):
        for kind in range(2):
            for part in range(2):
                series[kind, part, pl.ds(source * local, local)] = values[:, kind, part].astype(f32)

    unpack(me, green_out[me])
    for step in reversed(steps):
        other = partner(me, step)
        for energy in range(local):
            green_copy(other, other, energy).wait_recv()
        unpack(other, green_in[other])

    factor = 1.0 / math.sqrt(energies)

    def correlate(kind, owner):
        first_lag = owner * local

        def some_energies(index, sums):
            sum_real, sum_imag = sums
            start = index * local
            window = pl.ds(start + first_lag, 2 * local - 1)
            ahead_real, ahead_imag = series[kind, 0, window], series[kind, 1, window]
            for i in range(local):
                real, imag = series[1 - kind, 0, start + i], series[1 - kind, 1, start + i]
                shifted_real, shifted_imag = ahead_real[i : i + local], ahead_imag[i : i + local]
                sum_real = sum_real + (shifted_real * real + shifted_imag * imag)
                sum_imag = sum_imag + (shifted_imag * real - shifted_real * imag)
            return sum_real, sum_imag

        zero = jnp.zeros((local, ROWS, order), f32)
        sum_real, sum_imag = lax.fori_loop(0, peers - owner, some_energies, (zero, zero))
        return (sum_real * factor).astype(jnp.bfloat16), (sum_imag * factor).astype(jnp.bfloat16)

    def polar_copy(other, slot, kind):
        return pltpu.make_async_remote_copy(
            src_ref=polar_out.at[other, kind],
            dst_ref=polar_in.at[slot, kind],
            send_sem=polar_send.at[other, kind],
            recv_sem=polar_recv.at[slot, kind],
            device_id={"energy": other},
            device_id_type=MESH,
        )

    for kind in range(2):
        for step in steps:
            other = partner(me, step)
            real, imag = correlate(kind, other)
            polar_out[other, kind, :, 0] = real
            polar_out[other, kind, :, 1] = imag
            polar_copy(other, me, kind).start()
    for kind in range(2):
        real, imag = correlate(kind, me)
        polar_in[me, kind, :, 0] = real
        polar_in[me, kind, :, 1] = imag

    coulomb = coulomb_ref[0]
    for kind in range(2):
        for step in steps:
            other = partner(me, step)
            polar_copy(other, other, kind).wait_recv()
        for lag in range(local):
            both = jnp.concatenate(
                [polar_in[:, kind, lag, part].reshape(order, order) for part in range(2)], axis=1
            )
            left = jnp.dot(coulomb, both, preferred_element_type=f32).astype(jnp.bfloat16)
            tall = jnp.concatenate([left[:, :order], left[:, order:]], axis=0)
            screened = lax.dot_general(
                tall, coulomb, (((1,), (1,)), ((), ())), preferred_element_type=f32
            ).astype(jnp.bfloat16)
            out_ref[kind, 0, lag, 0] = screened[:order]
            out_ref[kind, 0, lag, 1] = screened[order:]

    for energy in range(local):

        @pl.when(has_next)
        def _():
            halo_copy(0, energy).wait_send()

        @pl.when(has_previous)
        def _():
            halo_copy(1, energy).wait_send()

        for step in steps:
            green_copy(partner(me, step), me, energy).wait_send()
    for kind in range(2):
        for step in steps:
            polar_copy(partner(me, step), me, kind).wait_send()


def fused_body(green_lower, green_diag, green_upper, self_energy, coulomb):
    peers, sites = lax.axis_size("energy"), lax.axis_size("space")
    local, order = green_diag.shape[1], green_diag.shape[-1]
    bf16 = jnp.bfloat16
    share = (peers, local, 2, 2, ROWS, order)
    lags = (peers, 2, local, 2, ROWS, order)
    dma = pltpu.SemaphoreType.DMA
    return pl.pallas_call(
        functools.partial(fused_kernel, peers, sites),
        out_shape=jax.ShapeDtypeStruct(self_energy.shape, bf16),
        in_specs=[pl.BlockSpec(memory_space=pltpu.VMEM)] * 5,
        out_specs=pl.BlockSpec(memory_space=pltpu.VMEM),
        scratch_shapes=[
            pltpu.VMEM((2, local, 2, 2, order, order), bf16),
            pltpu.VMEM(share, bf16),
            pltpu.VMEM(share, bf16),
            pltpu.VMEM((2, 2, peers * local + local, ROWS, order), jnp.float32),
            pltpu.VMEM(lags, bf16),
            pltpu.VMEM(lags, bf16),
            dma((2, local)),
            dma((2, local)),
            dma((peers, local)),
            dma((peers, local)),
            dma((peers, 2)),
            dma((peers, 2)),
        ],
        compiler_params=pltpu.CompilerParams(
            collective_id=0, has_side_effects=True, vmem_limit_bytes=40 * 2**20
        ),
    )(green_lower, green_diag, green_upper, self_energy, coulomb)


def body(green_lower, green_diag, green_upper, self_energy, coulomb):
    peers = lax.axis_size("energy")
    blocks, order = green_diag.shape[0], green_diag.shape[-1]
    if blocks == 1 and order == peers * ROWS and peers & (peers - 1) == 0:
        return fused_body(green_lower, green_diag, green_upper, self_energy, coulomb)
    return plain_body(green_lower, green_diag, green_upper, self_energy, coulomb)


def solution(mesh):
    in_specs = (
        P("space", "energy", None, None, None),
        P("space", "energy", None, None, None),
        P("space", "energy", None, None, None),
        P(None, "space", "energy", None, None, None),
        P("space", None, None),
    )
    out_specs = P(None, "space", "energy", None, None, None)
    return jax.shard_map(body, mesh=mesh, in_specs=in_specs, out_specs=out_specs, check_vma=False)
```

```python
import functools
import math

import jax
import jax.numpy as jnp
from jax import lax
from jax.experimental import pallas as pl
from jax.experimental.pallas import tpu as pltpu
from jax.sharding import PartitionSpec as P


def padded_2(shard, sides, width):
    for axis, dim in sides:
        peers, length = (lax.axis_size(axis), shard.shape[dim])
        up = [(i, (i + 1) % peers) for i in range(peers - 1)]
        down = [(j, i) for i, j in up]
        last = lax.slice_in_dim(shard, length - width, length, axis=dim)
        initial = lax.slice_in_dim(shard, 0, width, axis=dim)
        before = lax.ppermute(last, axis, up)
        after = lax.ppermute(initial, axis, down)
        shard = jnp.concatenate([before, shard, after], axis=dim)
    return shard


def congruence(green, sigma):
    green_real = green[:, :, 0]
    green_imag = green[:, :, 1]
    sigma_real = sigma[:, :, :, 0]
    sigma_imag = sigma[:, :, :, 1]
    green_wide = jnp.concatenate([green_real, green_imag], axis=-1)
    sigma_tall = jnp.concatenate(
        [
            jnp.concatenate([sigma_real, sigma_imag], axis=-1),
            jnp.concatenate([-sigma_imag, sigma_real], axis=-1),
        ],
        axis=-2,
    )
    mixed = jnp.einsum(
        "nepq,fneqr->fnepr", green_wide, sigma_tall, preferred_element_type=jnp.float32
    ).astype(jnp.bfloat16)
    adjoint_tall = jnp.concatenate(
        [green_wide, jnp.concatenate([-green_imag, green_real], axis=-1)], axis=-2
    )
    return jnp.einsum("fnepr,nesr->fneps", mixed, adjoint_tall, preferred_element_type=jnp.float32)


def split_table(table):
    high_part = table.astype(jnp.bfloat16)
    low_part = (table - high_part.astype(jnp.float32)).astype(jnp.bfloat16)
    return (high_part, low_part)


def spectrum(values, table_high, table_low, padded_len):

    def apply_table(part):
        return jnp.dot(table_high, part, preferred_element_type=jnp.float32) + jnp.dot(
            table_low, part, preferred_element_type=jnp.float32
        )

    real_terms = apply_table(values[:, 0])
    imag_terms = apply_table(values[:, 1])
    out_real = real_terms[:padded_len] + imag_terms[padded_len:]
    out_imag = imag_terms[:padded_len] - real_terms[padded_len:]
    return (out_real, out_imag)


def plain_body(green_lower, green_diag, green_upper, self_energy, coulomb):
    block_count = green_diag.shape[0]
    energy_local = green_diag.shape[1]
    block_order = green_diag.shape[-1]
    energies = energy_local * lax.axis_size("energy")
    padded_len = 2 * energies
    padded = padded_2(self_energy, (("space", 1),), 1)
    lower_term = congruence(green_lower, padded[:, :block_count])
    diag_term = congruence(green_diag, padded[:, 1 : block_count + 1])
    upper_term = congruence(green_upper, padded[:, 2:])
    total = lower_term + diag_term + upper_term
    total = total.reshape(2, block_count, energy_local, block_order, 2, block_order)
    green_function = (
        jnp.transpose(total, (0, 2, 4, 1, 3, 5))
        .astype(jnp.bfloat16)
        .reshape(2, energy_local, 2, -1)
    )
    frequency = lax.iota(jnp.int32, padded_len)
    energy_index = lax.iota(jnp.int32, energies)
    step_angle = 2.0 * math.pi / padded_len
    forward_angle = (frequency[:, None] * energy_index[None, :] % padded_len).astype(
        jnp.float32
    ) * step_angle
    forward_table = jnp.concatenate([jnp.cos(forward_angle), jnp.sin(forward_angle)], axis=0)
    table_high, table_low = split_table(forward_table)
    lesser_values = lax.all_to_all(
        green_function[0], "energy", split_axis=2, concat_axis=0, tiled=True
    )
    greater_values = lax.all_to_all(
        green_function[1], "energy", split_axis=2, concat_axis=0, tiled=True
    )
    lesser_real, lesser_imag = spectrum(lesser_values, table_high, table_low, padded_len)
    greater_real, greater_imag = spectrum(greater_values, table_high, table_low, padded_len)
    product_real = lesser_real * greater_real + lesser_imag * greater_imag
    product_imag = lesser_imag * greater_real - lesser_real * greater_imag
    row_index = jnp.concatenate([energy_index, (padded_len - energy_index) % padded_len])
    back_angle = (row_index[:, None] * frequency[None, :] % padded_len).astype(
        jnp.float32
    ) * step_angle
    back_cos = jnp.cos(back_angle)
    back_sin = jnp.sin(back_angle)
    back_table = jnp.concatenate(
        [
            jnp.concatenate([back_cos, -back_sin], axis=1),
            jnp.concatenate([back_sin, back_cos], axis=1),
        ],
        axis=0,
    )
    stacked_product = jnp.concatenate([product_real, product_imag], axis=0)
    factor = 1.0 / (padded_len * math.sqrt(energies))
    combined = (
        jnp.dot(
            back_table,
            stacked_product,
            precision=lax.Precision.HIGH,
            preferred_element_type=jnp.float32,
        )
        * factor
    )
    corr_real = combined[:padded_len]
    corr_imag = combined[padded_len:]
    lesser_lags = jnp.stack([corr_real[:energies], corr_imag[:energies]], axis=1)
    greater_lags = jnp.stack([corr_real[energies:], -corr_imag[energies:]], axis=1)
    polar = jnp.stack([lesser_lags, greater_lags], axis=0).astype(jnp.bfloat16)
    returned = lax.all_to_all(polar, "energy", split_axis=1, concat_axis=3, tiled=True)
    returned = returned.reshape(2, energy_local, 2, block_count, block_order, block_order)
    left_product = jnp.einsum(
        "npq,fetnqr->fetnpr", coulomb, returned, preferred_element_type=jnp.float32
    ).astype(jnp.bfloat16)
    screened = jnp.einsum(
        "fetnpr,nsr->fnetps", left_product, coulomb, preferred_element_type=jnp.float32
    )
    return screened.astype(jnp.bfloat16)


ROWS = 16
MESH = pl.DeviceIdType.MESH


def partner(me, step):
    other, bit = me, 1
    while bit <= step:
        if step & bit:
            other = other + bit * (1 - 2 * lax.rem(lax.div(me, bit), 2))
        bit *= 2
    return other


def far_first(peers):
    steps, span = [], peers // 2
    while span >= 1:
        steps += list(range(span, 2 * span))
        span //= 2
    return steps


def rotation(real, imag):
    return jnp.concatenate(
        [
            jnp.concatenate([real, imag], axis=1),
            jnp.concatenate([-imag, real], axis=1),
        ],
        axis=0,
    )


def fused_kernel(
    peers,
    sites,
    lower_hbm,
    diag_hbm,
    upper_hbm,
    sigma_hbm,
    coulomb_hbm,
    out_ref,
    lower_ref,
    diag_ref,
    upper_ref,
    sigma_ref,
    coulomb_ref,
    halo,
    green_out,
    green_in,
    series,
    polar_out,
    polar_in,
    load_sem,
    coulomb_sem,
    halo_send,
    halo_recv,
    green_send,
    green_recv,
    polar_send,
    polar_recv,
):
    me = lax.axis_index("energy")
    site = lax.axis_index("space")
    has_next = site < sites - 1
    has_previous = site > 0
    next_site = lax.rem(site + 1, sites)
    previous_site = lax.rem(site + sites - 1, sites)
    local, order = diag_ref.shape[0], diag_ref.shape[-1]
    half = order // 2
    energies = peers * local
    steps = far_first(peers)
    f32, bf16 = jnp.float32, jnp.bfloat16

    barrier = pltpu.get_barrier_semaphore()
    for step in steps:
        pl.semaphore_signal(
            barrier, inc=1, device_id={"energy": partner(me, step)}, device_id_type=MESH
        )

    @pl.when(has_next)
    def _():
        pl.semaphore_signal(barrier, inc=1, device_id={"space": next_site}, device_id_type=MESH)

    @pl.when(has_previous)
    def _():
        pl.semaphore_signal(barrier, inc=1, device_id={"space": previous_site}, device_id_type=MESH)

    def loads(energy):
        pairs = [
            (diag_hbm.at[0, energy], diag_ref.at[energy]),
            (sigma_hbm.at[:, 0, energy], sigma_ref.at[:, energy]),
            (lower_hbm.at[0, energy], lower_ref.at[energy]),
            (upper_hbm.at[0, energy], upper_ref.at[energy]),
        ]
        return [
            pltpu.make_async_copy(source, target, load_sem.at[energy, i])
            for i, (source, target) in enumerate(pairs)
        ]

    for energy in range(local):
        for load in loads(energy):
            load.start()
    coulomb_load = pltpu.make_async_copy(coulomb_hbm.at[0], coulomb_ref, coulomb_sem)
    coulomb_load.start()

    neighbours = jnp.where(has_next, 1, 0) + jnp.where(has_previous, 1, 0)
    pl.semaphore_wait(barrier, peers - 1 + neighbours)

    def halo_copy(side, energy):
        return pltpu.make_async_remote_copy(
            src_ref=sigma_hbm.at[:, 0, energy],
            dst_ref=halo.at[side, energy],
            send_sem=halo_send.at[side, energy],
            recv_sem=halo_recv.at[side, energy],
            device_id={"space": next_site if side == 0 else previous_site},
            device_id_type=MESH,
        )

    for energy in range(local):

        @pl.when(has_next)
        def _():
            halo_copy(0, energy).start()

        @pl.when(has_previous)
        def _():
            halo_copy(1, energy).start()

    @pl.when(jnp.logical_not(has_previous))
    def _():
        halo[0] = jnp.zeros(halo.shape[1:], halo.dtype)

    @pl.when(jnp.logical_not(has_next))
    def _():
        halo[1] = jnp.zeros(halo.shape[1:], halo.dtype)

    def green_copy(side, other, slot, first, count):
        return pltpu.make_async_remote_copy(
            src_ref=green_out.at[side, other, pl.ds(first, count)],
            dst_ref=green_in.at[side, slot, pl.ds(first, count)],
            send_sem=green_send.at[side, other, first],
            recv_sem=green_recv.at[side, slot, first],
            device_id={"energy": other},
            device_id_type=MESH,
        )

    parts = [
        [(energy, 1) for energy in range(local)],
        [(0, 1)] + ([(1, local - 1)] if local > 1 else []),
    ]

    def send_green(side, first, count):
        for step in steps:
            green_copy(side, partner(me, step), me, first, count).start()

    def term(green_ref, energy, sigma_of):
        real, imag = green_ref[energy, 0], green_ref[energy, 1]
        wide = jnp.concatenate([real, imag], axis=1)
        mixed = [
            jnp.dot(
                wide,
                rotation(sigma_of(kind, 0), sigma_of(kind, 1)),
                preferred_element_type=f32,
            ).astype(bf16)
            for kind in range(2)
        ]
        adjoint = jnp.concatenate(
            [rotation(real[:half], imag[:half]), rotation(real[half:], imag[half:])], axis=0
        )
        return lax.dot_general(
            jnp.concatenate(mixed, axis=0),
            adjoint,
            (((1,), (1,)), ((), ())),
            preferred_element_type=f32,
        )

    for energy in range(local):
        for load in loads(energy):
            load.wait()
        total = term(diag_ref, energy, lambda kind, part: sigma_ref[kind, energy, part])

        @pl.when(has_previous)
        def _():
            halo_copy(0, energy).wait_recv()

        @pl.when(has_next)
        def _():
            halo_copy(1, energy).wait_recv()

        total += term(lower_ref, energy, lambda kind, part: halo[0, energy, kind, part])
        total += term(upper_ref, energy, lambda kind, part: halo[1, energy, kind, part])
        rounded = total.astype(bf16)
        for side in range(2):
            for kind in range(2):
                block = rounded[
                    kind * order : (kind + 1) * order, side * order : (side + 1) * order
                ]
                green_out[side, :, energy, kind] = block.reshape(peers, ROWS, order)
        send_green(0, energy, 1)
        if energy == 0:
            send_green(1, 0, 1)
    if local > 1:
        send_green(1, *parts[1][1])

    coulomb_load.wait()
    coulomb = coulomb_ref[...]
    in_low = lax.broadcasted_iota(jnp.int32, (order, order), 1) < half
    straight = coulomb.astype(f32)
    swapped = pltpu.roll(straight, half, 1)
    zeros = jnp.zeros_like(straight)
    spread = jnp.concatenate(
        [
            jnp.concatenate(
                [jnp.where(in_low, straight, zeros), jnp.where(in_low, swapped, zeros)], axis=1
            ),
            jnp.concatenate(
                [jnp.where(in_low, zeros, swapped), jnp.where(in_low, zeros, straight)], axis=1
            ),
        ],
        axis=0,
    ).astype(bf16)

    fold = ROWS // 2
    low_lanes = lax.broadcasted_iota(jnp.int32, (local, fold, order), 2) < half

    def swap(values):
        return pltpu.roll(values.reshape(-1, order), half, 1).reshape(values.shape)

    tail = series.shape[3] - energies
    for side in range(2):
        for kind in range(2):
            for part in range(2):
                series[side, kind, part, energies:] = jnp.zeros((tail, fold, order), f32)

    def unpack(side, source, values):
        for kind in range(2):
            tile = values[:, kind].astype(f32)
            top, bottom = tile[:, :fold], tile[:, fold:]
            where = pl.ds(source * local, local)
            series[side, kind, 0, where] = jnp.where(low_lanes, top, swap(bottom))
            series[side, kind, 1, where] = jnp.where(low_lanes, swap(top), bottom)

    def receive_green(side):
        unpack(side, me, green_out[side, me])
        for step in steps:
            other = partner(me, step)
            for first, count in parts[side]:
                green_copy(side, other, other, first, count).wait_recv()
            unpack(side, other, green_in[side, other])

    factor = 1.0 / math.sqrt(energies)

    def correlate(side, owner):
        first_lag = owner * local

        def some_energies(index, sums):
            start = index * local
            window = pl.ds(start + first_lag, 2 * local - 1)
            results = []
            for kind in range(2):
                sum_real, sum_imag = sums[2 * kind : 2 * kind + 2]
                ahead_real, ahead_imag = series[side, kind, 0, window], series[side, kind, 1, window]
                for i in range(local):
                    real = series[side, 1 - kind, 0, start + i]
                    imag = series[side, 1 - kind, 1, start + i]
                    shifted_real, shifted_imag = ahead_real[i : i + local], ahead_imag[i : i + local]
                    sum_real = sum_real + (shifted_real * real + shifted_imag * imag)
                    sum_imag = sum_imag + (shifted_imag * real - shifted_real * imag)
                results += [sum_real, sum_imag]
            return tuple(results)

        zero = jnp.zeros((local, fold, order), f32)
        sums = lax.fori_loop(0, peers - owner, some_energies, (zero,) * 4)
        tiles = []
        for kind in range(2):
            real, imag = sums[2 * kind] * factor, sums[2 * kind + 1] * factor
            top = jnp.where(low_lanes, real, swap(imag))
            bottom = jnp.where(low_lanes, swap(real), imag)
            tiles.append(jnp.concatenate([top, bottom], axis=1).astype(bf16))
        return tiles

    def polar_copy(side, other, slot, kind):
        return pltpu.make_async_remote_copy(
            src_ref=polar_out.at[side, other, kind],
            dst_ref=polar_in.at[side, slot, kind],
            send_sem=polar_send.at[side, other, kind],
            recv_sem=polar_recv.at[side, slot, kind],
            device_id={"energy": other},
            device_id_type=MESH,
        )

    for side in range(2):
        receive_green(side)
        for step in steps:
            other = partner(me, step)
            tiles = correlate(side, other)
            for kind in range(2):
                polar_out[side, other, kind] = tiles[kind]
            for kind in range(2 if side == 0 else 1):
                polar_copy(side, other, me, kind).start()
        if side == 1:
            for step in steps:
                polar_copy(side, partner(me, step), me, 1).start()
        tiles = correlate(side, me)
        for kind in range(2):
            polar_in[side, me, kind] = tiles[kind]

    for kind in range(2):
        for side in range(2):
            for step in steps:
                other = partner(me, step)
                polar_copy(side, other, other, kind).wait_recv()
        lefts = []
        for lag in range(local):
            both = jnp.concatenate(
                [polar_in[side, :, kind, lag].reshape(order, order) for side in range(2)], axis=1
            )
            lefts.append(jnp.dot(coulomb, both, preferred_element_type=f32).astype(bf16))
        screened = lax.dot_general(
            jnp.concatenate(lefts, axis=0),
            spread,
            (((1,), (1,)), ((), ())),
            preferred_element_type=f32,
        ).astype(bf16)
        for lag in range(local):
            rows = screened[lag * order : (lag + 1) * order]
            out_ref[kind, 0, lag, 0] = rows[:, :order]
            out_ref[kind, 0, lag, 1] = rows[:, order:]

    for energy in range(local):

        @pl.when(has_next)
        def _():
            halo_copy(0, energy).wait_send()

        @pl.when(has_previous)
        def _():
            halo_copy(1, energy).wait_send()

    for side in range(2):
        for step in steps:
            other = partner(me, step)
            for first, count in parts[side]:
                green_copy(side, other, me, first, count).wait_send()
            for kind in range(2):
                polar_copy(side, other, me, kind).wait_send()


def fused_body(green_lower, green_diag, green_upper, self_energy, coulomb):
    peers, sites = lax.axis_size("energy"), lax.axis_size("space")
    local, order = green_diag.shape[1], green_diag.shape[-1]
    bf16 = jnp.bfloat16
    share = (2, peers, local, 2, ROWS, order)
    lags = (2, peers, 2, local, ROWS, order)
    series = (2, 2, 2, peers * local + local, ROWS // 2, order)
    dma = pltpu.SemaphoreType.DMA
    return pl.pallas_call(
        functools.partial(fused_kernel, peers, sites),
        out_shape=jax.ShapeDtypeStruct(self_energy.shape, bf16),
        in_specs=[pl.BlockSpec(memory_space=pltpu.HBM)] * 5,
        out_specs=pl.BlockSpec(memory_space=pltpu.VMEM),
        scratch_shapes=[pltpu.VMEM((local, 2, order, order), bf16)] * 3
        + [
            pltpu.VMEM((2, local, 2, order, order), bf16),
            pltpu.VMEM((order, order), bf16),
            pltpu.VMEM((2, local, 2, 2, order, order), bf16),
            pltpu.VMEM(share, bf16),
            pltpu.VMEM(share, bf16),
            pltpu.VMEM(series, jnp.float32),
            pltpu.VMEM(lags, bf16),
            pltpu.VMEM(lags, bf16),
            dma((local, 4)),
            dma,
            dma((2, local)),
            dma((2, local)),
            dma((2, peers, local)),
            dma((2, peers, local)),
            dma((2, peers, 2)),
            dma((2, peers, 2)),
        ],
        compiler_params=pltpu.CompilerParams(
            collective_id=0, has_side_effects=True, vmem_limit_bytes=40 * 2**20
        ),
    )(green_lower, green_diag, green_upper, self_energy, coulomb)


def body(green_lower, green_diag, green_upper, self_energy, coulomb):
    peers = lax.axis_size("energy")
    blocks, order = green_diag.shape[0], green_diag.shape[-1]
    if blocks == 1 and order == 128 and order == peers * ROWS and peers & (peers - 1) == 0:
        return fused_body(green_lower, green_diag, green_upper, self_energy, coulomb)
    return plain_body(green_lower, green_diag, green_upper, self_energy, coulomb)


def solution(mesh):
    in_specs = (
        P("space", "energy", None, None, None),
        P("space", "energy", None, None, None),
        P("space", "energy", None, None, None),
        P(None, "space", "energy", None, None, None),
        P("space", None, None),
    )
    out_specs = P(None, "space", "energy", None, None, None)
    return jax.shard_map(body, mesh=mesh, in_specs=in_specs, out_specs=out_specs, check_vma=False)
```

```python
import functools
import math

import jax
import jax.numpy as jnp
from jax import lax
from jax.experimental import pallas as pl
from jax.experimental.pallas import tpu as pltpu
from jax.sharding import PartitionSpec as P


def padded_2(shard, sides, width):
    for axis, dim in sides:
        peers, length = (lax.axis_size(axis), shard.shape[dim])
        up = [(i, (i + 1) % peers) for i in range(peers - 1)]
        down = [(j, i) for i, j in up]
        last = lax.slice_in_dim(shard, length - width, length, axis=dim)
        initial = lax.slice_in_dim(shard, 0, width, axis=dim)
        before = lax.ppermute(last, axis, up)
        after = lax.ppermute(initial, axis, down)
        shard = jnp.concatenate([before, shard, after], axis=dim)
    return shard


def congruence(green, sigma):
    green_real = green[:, :, 0]
    green_imag = green[:, :, 1]
    sigma_real = sigma[:, :, :, 0]
    sigma_imag = sigma[:, :, :, 1]
    green_wide = jnp.concatenate([green_real, green_imag], axis=-1)
    sigma_tall = jnp.concatenate(
        [
            jnp.concatenate([sigma_real, sigma_imag], axis=-1),
            jnp.concatenate([-sigma_imag, sigma_real], axis=-1),
        ],
        axis=-2,
    )
    mixed = jnp.einsum(
        "nepq,fneqr->fnepr", green_wide, sigma_tall, preferred_element_type=jnp.float32
    ).astype(jnp.bfloat16)
    adjoint_tall = jnp.concatenate(
        [green_wide, jnp.concatenate([-green_imag, green_real], axis=-1)], axis=-2
    )
    return jnp.einsum("fnepr,nesr->fneps", mixed, adjoint_tall, preferred_element_type=jnp.float32)


def split_table(table):
    high_part = table.astype(jnp.bfloat16)
    low_part = (table - high_part.astype(jnp.float32)).astype(jnp.bfloat16)
    return (high_part, low_part)


def spectrum(values, table_high, table_low, padded_len):

    def apply_table(part):
        return jnp.dot(table_high, part, preferred_element_type=jnp.float32) + jnp.dot(
            table_low, part, preferred_element_type=jnp.float32
        )

    real_terms = apply_table(values[:, 0])
    imag_terms = apply_table(values[:, 1])
    out_real = real_terms[:padded_len] + imag_terms[padded_len:]
    out_imag = imag_terms[:padded_len] - real_terms[padded_len:]
    return (out_real, out_imag)


def plain_body(green_lower, green_diag, green_upper, self_energy, coulomb):
    block_count = green_diag.shape[0]
    energy_local = green_diag.shape[1]
    block_order = green_diag.shape[-1]
    energies = energy_local * lax.axis_size("energy")
    padded_len = 2 * energies
    padded = padded_2(self_energy, (("space", 1),), 1)
    lower_term = congruence(green_lower, padded[:, :block_count])
    diag_term = congruence(green_diag, padded[:, 1 : block_count + 1])
    upper_term = congruence(green_upper, padded[:, 2:])
    total = lower_term + diag_term + upper_term
    total = total.reshape(2, block_count, energy_local, block_order, 2, block_order)
    green_function = (
        jnp.transpose(total, (0, 2, 4, 1, 3, 5))
        .astype(jnp.bfloat16)
        .reshape(2, energy_local, 2, -1)
    )
    frequency = lax.iota(jnp.int32, padded_len)
    energy_index = lax.iota(jnp.int32, energies)
    step_angle = 2.0 * math.pi / padded_len
    forward_angle = (frequency[:, None] * energy_index[None, :] % padded_len).astype(
        jnp.float32
    ) * step_angle
    forward_table = jnp.concatenate([jnp.cos(forward_angle), jnp.sin(forward_angle)], axis=0)
    table_high, table_low = split_table(forward_table)
    lesser_values = lax.all_to_all(
        green_function[0], "energy", split_axis=2, concat_axis=0, tiled=True
    )
    greater_values = lax.all_to_all(
        green_function[1], "energy", split_axis=2, concat_axis=0, tiled=True
    )
    lesser_real, lesser_imag = spectrum(lesser_values, table_high, table_low, padded_len)
    greater_real, greater_imag = spectrum(greater_values, table_high, table_low, padded_len)
    product_real = lesser_real * greater_real + lesser_imag * greater_imag
    product_imag = lesser_imag * greater_real - lesser_real * greater_imag
    row_index = jnp.concatenate([energy_index, (padded_len - energy_index) % padded_len])
    back_angle = (row_index[:, None] * frequency[None, :] % padded_len).astype(
        jnp.float32
    ) * step_angle
    back_cos = jnp.cos(back_angle)
    back_sin = jnp.sin(back_angle)
    back_table = jnp.concatenate(
        [
            jnp.concatenate([back_cos, -back_sin], axis=1),
            jnp.concatenate([back_sin, back_cos], axis=1),
        ],
        axis=0,
    )
    stacked_product = jnp.concatenate([product_real, product_imag], axis=0)
    factor = 1.0 / (padded_len * math.sqrt(energies))
    combined = (
        jnp.dot(
            back_table,
            stacked_product,
            precision=lax.Precision.HIGH,
            preferred_element_type=jnp.float32,
        )
        * factor
    )
    corr_real = combined[:padded_len]
    corr_imag = combined[padded_len:]
    lesser_lags = jnp.stack([corr_real[:energies], corr_imag[:energies]], axis=1)
    greater_lags = jnp.stack([corr_real[energies:], -corr_imag[energies:]], axis=1)
    polar = jnp.stack([lesser_lags, greater_lags], axis=0).astype(jnp.bfloat16)
    returned = lax.all_to_all(polar, "energy", split_axis=1, concat_axis=3, tiled=True)
    returned = returned.reshape(2, energy_local, 2, block_count, block_order, block_order)
    left_product = jnp.einsum(
        "npq,fetnqr->fetnpr", coulomb, returned, preferred_element_type=jnp.float32
    ).astype(jnp.bfloat16)
    screened = jnp.einsum(
        "fetnpr,nsr->fnetps", left_product, coulomb, preferred_element_type=jnp.float32
    )
    return screened.astype(jnp.bfloat16)


ROWS = 16
MESH = pl.DeviceIdType.MESH


def partner(me, step):
    other, bit = me, 1
    while bit <= step:
        if step & bit:
            other = other + bit * (1 - 2 * lax.rem(lax.div(me, bit), 2))
        bit *= 2
    return other


def far_first(peers):
    steps, span = [], peers // 2
    while span >= 1:
        steps += list(range(span, 2 * span))
        span //= 2
    return steps


def rotation(real, imag):
    return jnp.concatenate(
        [
            jnp.concatenate([real, imag], axis=1),
            jnp.concatenate([-imag, real], axis=1),
        ],
        axis=0,
    )


def fused_kernel(
    peers,
    sites,
    lower_hbm,
    diag_hbm,
    upper_hbm,
    sigma_hbm,
    coulomb_hbm,
    out_hbm,
    lower_ref,
    diag_ref,
    upper_ref,
    sigma_ref,
    coulomb_ref,
    halo,
    total,
    green_out,
    green_in,
    series,
    polar_out,
    polar_in,
    out_ref,
    out_sem,
    load_sem,
    coulomb_sem,
    halo_send,
    halo_recv,
    green_send,
    green_recv,
    polar_send,
    polar_recv,
):
    me = lax.axis_index("energy")
    site = lax.axis_index("space")
    has_next = site < sites - 1
    has_previous = site > 0
    next_site = lax.rem(site + 1, sites)
    previous_site = lax.rem(site + sites - 1, sites)
    local, order = diag_ref.shape[0], diag_ref.shape[-1]
    half = order // 2
    energies = peers * local
    steps = far_first(peers)
    f32, bf16 = jnp.float32, jnp.bfloat16

    barrier = pltpu.get_barrier_semaphore()
    for step in steps:
        pl.semaphore_signal(
            barrier, inc=1, device_id={"energy": partner(me, step)}, device_id_type=MESH
        )

    @pl.when(has_next)
    def _():
        pl.semaphore_signal(barrier, inc=1, device_id={"space": next_site}, device_id_type=MESH)

    @pl.when(has_previous)
    def _():
        pl.semaphore_signal(barrier, inc=1, device_id={"space": previous_site}, device_id_type=MESH)

    def loads(energy):
        pairs = [
            (diag_hbm.at[0, energy], diag_ref.at[energy]),
            (sigma_hbm.at[:, 0, energy], sigma_ref.at[:, energy]),
            (lower_hbm.at[0, energy], lower_ref.at[energy]),
            (upper_hbm.at[0, energy], upper_ref.at[energy]),
        ]
        return [
            pltpu.make_async_copy(source, target, load_sem.at[energy, i])
            for i, (source, target) in enumerate(pairs)
        ]

    for energy in range(local):
        for load in loads(energy):
            load.start()
    coulomb_load = pltpu.make_async_copy(coulomb_hbm.at[0], coulomb_ref, coulomb_sem)
    coulomb_load.start()

    neighbours = jnp.where(has_next, 1, 0) + jnp.where(has_previous, 1, 0)
    pl.semaphore_wait(barrier, peers - 1 + neighbours)

    def halo_copy(side, energy):
        return pltpu.make_async_remote_copy(
            src_ref=sigma_hbm.at[:, 0, energy],
            dst_ref=halo.at[side, energy],
            send_sem=halo_send.at[side, energy],
            recv_sem=halo_recv.at[side, energy],
            device_id={"space": next_site if side == 0 else previous_site},
            device_id_type=MESH,
        )

    def each_halo(energy, act):
        @pl.when(has_next)
        def _():
            act(halo_copy(0, energy))

        @pl.when(has_previous)
        def _():
            act(halo_copy(1, energy))

    for energy in range(min(2, local)):
        each_halo(energy, lambda copy: copy.start())

    @pl.when(jnp.logical_not(has_previous))
    def _():
        halo[0] = jnp.zeros(halo.shape[1:], halo.dtype)

    @pl.when(jnp.logical_not(has_next))
    def _():
        halo[1] = jnp.zeros(halo.shape[1:], halo.dtype)

    def green_copy(side, other, slot, first, count):
        return pltpu.make_async_remote_copy(
            src_ref=green_out.at[side, other, pl.ds(first, count)],
            dst_ref=green_in.at[side, slot, pl.ds(first, count)],
            send_sem=green_send.at[side, other, first],
            recv_sem=green_recv.at[side, slot, first],
            device_id={"energy": other},
            device_id_type=MESH,
        )

    parts = [
        [(energy, 1) for energy in range(local)],
        [(0, 1)] + ([(1, local - 1)] if local > 1 else []),
    ]

    def send_green(side, first, count):
        for step in steps:
            green_copy(side, partner(me, step), me, first, count).start()

    def term(energy, sources):
        mixed, adjoint = [], []
        for green_ref, sigma_of in sources:
            real, imag = green_ref[energy, 0], green_ref[energy, 1]
            wide = jnp.concatenate([real, imag], axis=1)
            mixed.append(
                jnp.concatenate(
                    [
                        jnp.dot(
                            wide,
                            rotation(sigma_of(kind, 0), sigma_of(kind, 1)),
                            preferred_element_type=f32,
                        ).astype(bf16)
                        for kind in range(2)
                    ],
                    axis=0,
                )
            )
            adjoint.append(
                jnp.concatenate(
                    [rotation(real[:half], imag[:half]), rotation(real[half:], imag[half:])],
                    axis=0,
                )
            )
        return lax.dot_general(
            jnp.concatenate(mixed, axis=1),
            jnp.concatenate(adjoint, axis=1),
            (((1,), (1,)), ((), ())),
            preferred_element_type=f32,
        )

    def own_term(energy):
        for load in loads(energy):
            load.wait()
        total[energy] = term(
            energy, [(diag_ref, lambda kind, part: sigma_ref[kind, energy, part])]
        )

    for energy in range(min(2, local)):
        own_term(energy)
    for energy in range(local):

        @pl.when(has_previous)
        def _():
            halo_copy(0, energy).wait_recv()

        @pl.when(has_next)
        def _():
            halo_copy(1, energy).wait_recv()

        each_halo(energy, lambda copy: copy.wait_send())
        if energy + 2 < local:
            each_halo(energy + 2, lambda copy: copy.start())
        coupled = term(
            energy,
            [
                (lower_ref, lambda kind, part: halo[0, energy, kind, part]),
                (upper_ref, lambda kind, part: halo[1, energy, kind, part]),
            ],
        )
        rounded = (total[energy] + coupled).astype(bf16)
        for side in range(2):
            for kind in range(2):
                block = rounded[
                    kind * order : (kind + 1) * order, side * order : (side + 1) * order
                ]
                green_out[side, :, energy, kind] = block.reshape(peers, ROWS, order)
        send_green(0, energy, 1)
        if energy == 0:
            send_green(1, 0, 1)
        if energy + 2 < local:
            own_term(energy + 2)
    if local > 1:
        send_green(1, *parts[1][1])

    coulomb_load.wait()
    coulomb = coulomb_ref[...]
    in_low = lax.broadcasted_iota(jnp.int32, (order, order), 1) < half
    straight = coulomb.astype(f32)
    swapped = pltpu.roll(straight, half, 1)
    zeros = jnp.zeros_like(straight)
    spread = jnp.concatenate(
        [
            jnp.concatenate(
                [jnp.where(in_low, straight, zeros), jnp.where(in_low, swapped, zeros)], axis=1
            ),
            jnp.concatenate(
                [jnp.where(in_low, zeros, swapped), jnp.where(in_low, zeros, straight)], axis=1
            ),
        ],
        axis=0,
    ).astype(bf16)

    fold = ROWS // 2
    low_lanes = lax.broadcasted_iota(jnp.int32, (local, fold, order), 2) < half

    def swap(values):
        return pltpu.roll(values.reshape(-1, order), half, 1).reshape(values.shape)

    tail = series.shape[3] - energies
    for side in range(2):
        for kind in range(2):
            for part in range(2):
                series[side, kind, part, energies:] = jnp.zeros((tail, fold, order), f32)

    def unpack(side, source, values):
        for kind in range(2):
            tile = values[:, kind].astype(f32)
            top, bottom = tile[:, :fold], tile[:, fold:]
            where = pl.ds(source * local, local)
            series[side, kind, 0, where] = jnp.where(low_lanes, top, swap(bottom))
            series[side, kind, 1, where] = jnp.where(low_lanes, swap(top), bottom)

    def receive_green(side):
        unpack(side, me, green_out[side, me])
        for step in steps:
            other = partner(me, step)
            for first, count in parts[side]:
                green_copy(side, other, other, first, count).wait_recv()
            unpack(side, other, green_in[side, other])

    factor = 1.0 / math.sqrt(energies)

    def correlate(side, owner):
        first_lag = owner * local

        def some_energies(index, sums):
            start = index * local
            window = pl.ds(start + first_lag, 2 * local - 1)
            results = []
            for kind in range(2):
                sum_real, sum_imag = sums[2 * kind : 2 * kind + 2]
                ahead_real, ahead_imag = series[side, kind, 0, window], series[side, kind, 1, window]
                for i in range(local):
                    real = series[side, 1 - kind, 0, start + i]
                    imag = series[side, 1 - kind, 1, start + i]
                    shifted_real, shifted_imag = ahead_real[i : i + local], ahead_imag[i : i + local]
                    sum_real = sum_real + (shifted_real * real + shifted_imag * imag)
                    sum_imag = sum_imag + (shifted_imag * real - shifted_real * imag)
                results += [sum_real, sum_imag]
            return tuple(results)

        zero = jnp.zeros((local, fold, order), f32)
        sums = lax.fori_loop(0, peers - owner, some_energies, (zero,) * 4)
        tiles = []
        for kind in range(2):
            real, imag = sums[2 * kind] * factor, sums[2 * kind + 1] * factor
            top = jnp.where(low_lanes, real, swap(imag))
            bottom = jnp.where(low_lanes, swap(real), imag)
            tiles.append(jnp.concatenate([top, bottom], axis=1).astype(bf16))
        return tiles

    def polar_copy(side, other, slot, kind):
        return pltpu.make_async_remote_copy(
            src_ref=polar_out.at[side, other, kind],
            dst_ref=polar_in.at[side, slot, kind],
            send_sem=polar_send.at[side, other, kind],
            recv_sem=polar_recv.at[side, slot, kind],
            device_id={"energy": other},
            device_id_type=MESH,
        )

    for side in range(2):
        receive_green(side)
        for step in steps:
            other = partner(me, step)
            tiles = correlate(side, other)
            for kind in range(2):
                polar_out[side, other, kind] = tiles[kind]
            for kind in range(2 if side == 0 else 1):
                polar_copy(side, other, me, kind).start()
        if side == 1:
            for step in steps:
                polar_copy(side, partner(me, step), me, 1).start()
        tiles = correlate(side, me)
        for kind in range(2):
            polar_in[side, me, kind] = tiles[kind]

    def out_copy(kind):
        return pltpu.make_async_copy(out_ref.at[kind], out_hbm.at[kind, 0], out_sem.at[kind])

    for kind in range(2):
        for side in range(2):
            for step in steps:
                other = partner(me, step)
                polar_copy(side, other, other, kind).wait_recv()
        lefts = []
        for lag in range(local):
            both = jnp.concatenate(
                [polar_in[side, :, kind, lag].reshape(order, order) for side in range(2)], axis=1
            )
            lefts.append(jnp.dot(coulomb, both, preferred_element_type=f32).astype(bf16))
        screened = lax.dot_general(
            jnp.concatenate(lefts, axis=0),
            spread,
            (((1,), (1,)), ((), ())),
            preferred_element_type=f32,
        ).astype(bf16)
        for lag in range(local):
            rows = screened[lag * order : (lag + 1) * order]
            out_ref[kind, lag, 0] = rows[:, :order]
            out_ref[kind, lag, 1] = rows[:, order:]
        out_copy(kind).start()

    for side in range(2):
        for step in steps:
            other = partner(me, step)
            for first, count in parts[side]:
                green_copy(side, other, me, first, count).wait_send()
            for kind in range(2):
                polar_copy(side, other, me, kind).wait_send()
    for kind in range(2):
        out_copy(kind).wait()


def fused_body(green_lower, green_diag, green_upper, self_energy, coulomb):
    peers, sites = lax.axis_size("energy"), lax.axis_size("space")
    local, order = green_diag.shape[1], green_diag.shape[-1]
    bf16 = jnp.bfloat16
    share = (2, peers, local, 2, ROWS, order)
    lags = (2, peers, 2, local, ROWS, order)
    series = (2, 2, 2, peers * local + local, ROWS // 2, order)
    dma = pltpu.SemaphoreType.DMA
    return pl.pallas_call(
        functools.partial(fused_kernel, peers, sites),
        out_shape=jax.ShapeDtypeStruct(self_energy.shape, bf16),
        in_specs=[pl.BlockSpec(memory_space=pltpu.HBM)] * 5,
        out_specs=pl.BlockSpec(memory_space=pltpu.HBM),
        scratch_shapes=[pltpu.VMEM((local, 2, order, order), bf16)] * 3
        + [
            pltpu.VMEM((2, local, 2, order, order), bf16),
            pltpu.VMEM((order, order), bf16),
            pltpu.VMEM((2, local, 2, 2, order, order), bf16),
            pltpu.VMEM((local, 2 * order, 2 * order), jnp.float32),
            pltpu.VMEM(share, bf16),
            pltpu.VMEM(share, bf16),
            pltpu.VMEM(series, jnp.float32),
            pltpu.VMEM(lags, bf16),
            pltpu.VMEM(lags, bf16),
            pltpu.VMEM((2, local, 2, order, order), bf16),
            dma((2,)),
            dma((local, 4)),
            dma,
            dma((2, local)),
            dma((2, local)),
            dma((2, peers, local)),
            dma((2, peers, local)),
            dma((2, peers, 2)),
            dma((2, peers, 2)),
        ],
        compiler_params=pltpu.CompilerParams(
            collective_id=0, has_side_effects=True, vmem_limit_bytes=64 * 2**20 - 2**15
        ),
    )(green_lower, green_diag, green_upper, self_energy, coulomb)


def body(green_lower, green_diag, green_upper, self_energy, coulomb):
    peers = lax.axis_size("energy")
    blocks, order = green_diag.shape[0], green_diag.shape[-1]
    if blocks == 1 and order == 128 and order == peers * ROWS and peers & (peers - 1) == 0:
        return fused_body(green_lower, green_diag, green_upper, self_energy, coulomb)
    return plain_body(green_lower, green_diag, green_upper, self_energy, coulomb)


def solution(mesh):
    in_specs = (
        P("space", "energy", None, None, None),
        P("space", "energy", None, None, None),
        P("space", "energy", None, None, None),
        P(None, "space", "energy", None, None, None),
        P("space", None, None),
    )
    out_specs = P(None, "space", "energy", None, None, None)
    return jax.shard_map(body, mesh=mesh, in_specs=in_specs, out_specs=out_specs, check_vma=False)
```

```python
import functools
import math

import jax
import jax.numpy as jnp
from jax import lax
from jax.experimental import pallas as pl
from jax.experimental.pallas import tpu as pltpu
from jax.sharding import PartitionSpec as P


def padded_2(shard, sides, width):
    for axis, dim in sides:
        peers, length = (lax.axis_size(axis), shard.shape[dim])
        up = [(i, (i + 1) % peers) for i in range(peers - 1)]
        down = [(j, i) for i, j in up]
        last = lax.slice_in_dim(shard, length - width, length, axis=dim)
        initial = lax.slice_in_dim(shard, 0, width, axis=dim)
        before = lax.ppermute(last, axis, up)
        after = lax.ppermute(initial, axis, down)
        shard = jnp.concatenate([before, shard, after], axis=dim)
    return shard


def congruence(green, sigma):
    green_real = green[:, :, 0]
    green_imag = green[:, :, 1]
    sigma_real = sigma[:, :, :, 0]
    sigma_imag = sigma[:, :, :, 1]
    green_wide = jnp.concatenate([green_real, green_imag], axis=-1)
    sigma_tall = jnp.concatenate(
        [
            jnp.concatenate([sigma_real, sigma_imag], axis=-1),
            jnp.concatenate([-sigma_imag, sigma_real], axis=-1),
        ],
        axis=-2,
    )
    mixed = jnp.einsum(
        "nepq,fneqr->fnepr", green_wide, sigma_tall, preferred_element_type=jnp.float32
    ).astype(jnp.bfloat16)
    adjoint_tall = jnp.concatenate(
        [green_wide, jnp.concatenate([-green_imag, green_real], axis=-1)], axis=-2
    )
    return jnp.einsum("fnepr,nesr->fneps", mixed, adjoint_tall, preferred_element_type=jnp.float32)


def split_table(table):
    high_part = table.astype(jnp.bfloat16)
    low_part = (table - high_part.astype(jnp.float32)).astype(jnp.bfloat16)
    return (high_part, low_part)


def spectrum(values, table_high, table_low, padded_len):

    def apply_table(part):
        return jnp.dot(table_high, part, preferred_element_type=jnp.float32) + jnp.dot(
            table_low, part, preferred_element_type=jnp.float32
        )

    real_terms = apply_table(values[:, 0])
    imag_terms = apply_table(values[:, 1])
    out_real = real_terms[:padded_len] + imag_terms[padded_len:]
    out_imag = imag_terms[:padded_len] - real_terms[padded_len:]
    return (out_real, out_imag)


def plain_body(green_lower, green_diag, green_upper, self_energy, coulomb):
    block_count = green_diag.shape[0]
    energy_local = green_diag.shape[1]
    block_order = green_diag.shape[-1]
    energies = energy_local * lax.axis_size("energy")
    padded_len = 2 * energies
    padded = padded_2(self_energy, (("space", 1),), 1)
    lower_term = congruence(green_lower, padded[:, :block_count])
    diag_term = congruence(green_diag, padded[:, 1 : block_count + 1])
    upper_term = congruence(green_upper, padded[:, 2:])
    total = lower_term + diag_term + upper_term
    total = total.reshape(2, block_count, energy_local, block_order, 2, block_order)
    green_function = (
        jnp.transpose(total, (0, 2, 4, 1, 3, 5))
        .astype(jnp.bfloat16)
        .reshape(2, energy_local, 2, -1)
    )
    frequency = lax.iota(jnp.int32, padded_len)
    energy_index = lax.iota(jnp.int32, energies)
    step_angle = 2.0 * math.pi / padded_len
    forward_angle = (frequency[:, None] * energy_index[None, :] % padded_len).astype(
        jnp.float32
    ) * step_angle
    forward_table = jnp.concatenate([jnp.cos(forward_angle), jnp.sin(forward_angle)], axis=0)
    table_high, table_low = split_table(forward_table)
    lesser_values = lax.all_to_all(
        green_function[0], "energy", split_axis=2, concat_axis=0, tiled=True
    )
    greater_values = lax.all_to_all(
        green_function[1], "energy", split_axis=2, concat_axis=0, tiled=True
    )
    lesser_real, lesser_imag = spectrum(lesser_values, table_high, table_low, padded_len)
    greater_real, greater_imag = spectrum(greater_values, table_high, table_low, padded_len)
    product_real = lesser_real * greater_real + lesser_imag * greater_imag
    product_imag = lesser_imag * greater_real - lesser_real * greater_imag
    row_index = jnp.concatenate([energy_index, (padded_len - energy_index) % padded_len])
    back_angle = (row_index[:, None] * frequency[None, :] % padded_len).astype(
        jnp.float32
    ) * step_angle
    back_cos = jnp.cos(back_angle)
    back_sin = jnp.sin(back_angle)
    back_table = jnp.concatenate(
        [
            jnp.concatenate([back_cos, -back_sin], axis=1),
            jnp.concatenate([back_sin, back_cos], axis=1),
        ],
        axis=0,
    )
    stacked_product = jnp.concatenate([product_real, product_imag], axis=0)
    factor = 1.0 / (padded_len * math.sqrt(energies))
    combined = (
        jnp.dot(
            back_table,
            stacked_product,
            precision=lax.Precision.HIGH,
            preferred_element_type=jnp.float32,
        )
        * factor
    )
    corr_real = combined[:padded_len]
    corr_imag = combined[padded_len:]
    lesser_lags = jnp.stack([corr_real[:energies], corr_imag[:energies]], axis=1)
    greater_lags = jnp.stack([corr_real[energies:], -corr_imag[energies:]], axis=1)
    polar = jnp.stack([lesser_lags, greater_lags], axis=0).astype(jnp.bfloat16)
    returned = lax.all_to_all(polar, "energy", split_axis=1, concat_axis=3, tiled=True)
    returned = returned.reshape(2, energy_local, 2, block_count, block_order, block_order)
    left_product = jnp.einsum(
        "npq,fetnqr->fetnpr", coulomb, returned, preferred_element_type=jnp.float32
    ).astype(jnp.bfloat16)
    screened = jnp.einsum(
        "fetnpr,nsr->fnetps", left_product, coulomb, preferred_element_type=jnp.float32
    )
    return screened.astype(jnp.bfloat16)


ROWS = 16
MESH = pl.DeviceIdType.MESH


def partner(me, step):
    other, bit = me, 1
    while bit <= step:
        if step & bit:
            other = other + bit * (1 - 2 * lax.rem(lax.div(me, bit), 2))
        bit *= 2
    return other


def alternate(peers):
    far, near = list(range(peers // 2, peers)), list(range(1, peers // 2))
    steps = []
    for i in range(peers // 2):
        steps += far[i : i + 1] + near[i : i + 1]
    return steps


def rotation(real, imag):
    return jnp.concatenate(
        [
            jnp.concatenate([real, imag], axis=1),
            jnp.concatenate([-imag, real], axis=1),
        ],
        axis=0,
    )


def fused_kernel(
    peers,
    sites,
    lower_hbm,
    diag_hbm,
    upper_hbm,
    sigma_hbm,
    coulomb_hbm,
    out_hbm,
    greens,
    sigma_ref,
    coulomb_ref,
    halo,
    total,
    green_out,
    green_in,
    series,
    polar_out,
    polar_in,
    out_ref,
    out_sem,
    load_sem,
    coulomb_sem,
    halo_send,
    halo_recv,
    green_send,
    green_recv,
    polar_send,
    polar_recv,
):
    me = lax.axis_index("energy")
    site = lax.axis_index("space")
    has_next = site < sites - 1
    has_previous = site > 0
    next_site = lax.rem(site + 1, sites)
    previous_site = lax.rem(site + sites - 1, sites)
    local, order = greens.shape[0], greens.shape[-1]
    half = order // 2
    energies = peers * local
    steps = alternate(peers)
    f32, bf16 = jnp.float32, jnp.bfloat16

    barrier = pltpu.get_barrier_semaphore()
    for step in steps:
        pl.semaphore_signal(
            barrier, inc=1, device_id={"energy": partner(me, step)}, device_id_type=MESH
        )

    @pl.when(has_next)
    def _():
        pl.semaphore_signal(barrier, inc=1, device_id={"space": next_site}, device_id_type=MESH)

    @pl.when(has_previous)
    def _():
        pl.semaphore_signal(barrier, inc=1, device_id={"space": previous_site}, device_id_type=MESH)

    def load_sigma(energy):
        return pltpu.make_async_copy(
            sigma_hbm.at[:, 0, energy], sigma_ref.at[:, energy], load_sem.at[energy, 0]
        )

    sources = (diag_hbm, lower_hbm, upper_hbm)
    for energy in range(local):
        load_sigma(energy).start()
        for i, source in enumerate(sources):
            pltpu.make_async_copy(
                source.at[0, energy], greens.at[energy, i], load_sem.at[energy, 1]
            ).start()
    coulomb_load = pltpu.make_async_copy(coulomb_hbm.at[0], coulomb_ref, coulomb_sem)
    coulomb_load.start()

    neighbours = jnp.where(has_next, 1, 0) + jnp.where(has_previous, 1, 0)
    pl.semaphore_wait(barrier, peers - 1 + neighbours)

    def halo_copy(side, energy):
        return pltpu.make_async_remote_copy(
            src_ref=sigma_hbm.at[:, 0, energy],
            dst_ref=halo.at[side, energy],
            send_sem=halo_send.at[side, energy],
            recv_sem=halo_recv.at[side, energy],
            device_id={"space": next_site if side == 0 else previous_site},
            device_id_type=MESH,
        )

    def each_halo(energy, act):
        @pl.when(has_next)
        def _():
            act(halo_copy(0, energy))

        @pl.when(has_previous)
        def _():
            act(halo_copy(1, energy))

    for energy in range(min(2, local)):
        each_halo(energy, lambda copy: copy.start())

    @pl.when(jnp.logical_not(has_previous))
    def _():
        halo[0] = jnp.zeros(halo.shape[1:], halo.dtype)

    @pl.when(jnp.logical_not(has_next))
    def _():
        halo[1] = jnp.zeros(halo.shape[1:], halo.dtype)

    def green_copy(side, other, slot, first, count):
        return pltpu.make_async_remote_copy(
            src_ref=green_out.at[side, other, pl.ds(first, count)],
            dst_ref=green_in.at[side, slot, pl.ds(first, count)],
            send_sem=green_send,
            recv_sem=green_recv.at[side, slot],
            device_id={"energy": other},
            device_id_type=MESH,
        )

    def send_green(side, first, count):
        for step in steps:
            green_copy(side, partner(me, step), me, first, count).start()

    def term(energy, terms):
        mixed, adjoint = [], []
        for which, sigma_of in terms:
            real, imag = greens[energy, which, 0], greens[energy, which, 1]
            wide = jnp.concatenate([real, imag], axis=1)
            mixed.append(
                jnp.concatenate(
                    [
                        jnp.dot(
                            wide,
                            rotation(sigma_of(kind, 0), sigma_of(kind, 1)),
                            preferred_element_type=f32,
                        ).astype(bf16)
                        for kind in range(2)
                    ],
                    axis=0,
                )
            )
            adjoint.append(
                jnp.concatenate(
                    [rotation(real[:half], imag[:half]), rotation(real[half:], imag[half:])],
                    axis=0,
                )
            )
        return lax.dot_general(
            jnp.concatenate(mixed, axis=1),
            jnp.concatenate(adjoint, axis=1),
            (((1,), (1,)), ((), ())),
            preferred_element_type=f32,
        )

    def own_term(energy):
        load_sigma(energy).wait()
        pltpu.make_async_copy(greens.at[energy], greens.at[energy], load_sem.at[energy, 1]).wait()
        total[energy] = term(energy, [(0, lambda kind, part: sigma_ref[kind, energy, part])])

    for energy in range(min(2, local)):
        own_term(energy)
    for energy in range(local):

        @pl.when(has_previous)
        def _():
            halo_copy(0, energy).wait_recv()

        @pl.when(has_next)
        def _():
            halo_copy(1, energy).wait_recv()

        each_halo(energy, lambda copy: copy.wait_send())
        if energy + 2 < local:
            each_halo(energy + 2, lambda copy: copy.start())
        coupled = term(
            energy,
            [
                (1, lambda kind, part: halo[0, energy, kind, part]),
                (2, lambda kind, part: halo[1, energy, kind, part]),
            ],
        )
        rounded = (total[energy] + coupled).astype(bf16)
        for side in range(2):
            for kind in range(2):
                block = rounded[
                    kind * order : (kind + 1) * order, side * order : (side + 1) * order
                ]
                green_out[side, :, energy, kind] = block.reshape(peers, ROWS, order)
        first = energy - energy % 2
        if energy % 2 == 1 or energy == local - 1:
            for side in range(2):
                send_green(side, first, energy + 1 - first)
        if energy + 2 < local:
            own_term(energy + 2)

    coulomb_load.wait()
    coulomb = coulomb_ref[...]
    in_low = lax.broadcasted_iota(jnp.int32, (order, order), 1) < half
    straight = coulomb.astype(f32)
    swapped = pltpu.roll(straight, half, 1)
    zeros = jnp.zeros_like(straight)
    spread = jnp.concatenate(
        [
            jnp.concatenate(
                [jnp.where(in_low, straight, zeros), jnp.where(in_low, swapped, zeros)], axis=1
            ),
            jnp.concatenate(
                [jnp.where(in_low, zeros, swapped), jnp.where(in_low, zeros, straight)], axis=1
            ),
        ],
        axis=0,
    ).astype(bf16)

    fold = ROWS // 2
    low_lanes = lax.broadcasted_iota(jnp.int32, (local, fold, order), 2) < half

    def swap(values):
        return pltpu.roll(values.reshape(-1, order), half, 1).reshape(values.shape)

    tail = series.shape[3] - energies
    for side in range(2):
        for kind in range(2):
            for part in range(2):
                series[side, kind, part, energies:] = jnp.zeros((tail, fold, order), f32)

    def unpack(side, source, values):
        for kind in range(2):
            tile = values[:, kind].astype(f32)
            top, bottom = tile[:, :fold], tile[:, fold:]
            where = pl.ds(source * local, local)
            series[side, kind, 0, where] = jnp.where(low_lanes, top, swap(bottom))
            series[side, kind, 1, where] = jnp.where(low_lanes, swap(top), bottom)

    def receive_green(side):
        unpack(side, me, green_out[side, me])
        for step in steps:
            other = partner(me, step)
            green_copy(side, other, other, 0, local).wait_recv()
            unpack(side, other, green_in[side, other])

    factor = 1.0 / math.sqrt(energies)

    def correlate(side, owner):
        first_lag = owner * local

        def some_energies(index, sums):
            start = index * local
            window = pl.ds(start + first_lag, 2 * local - 1)
            results = []
            for kind in range(2):
                sum_real, sum_imag = sums[2 * kind : 2 * kind + 2]
                ahead_real, ahead_imag = series[side, kind, 0, window], series[side, kind, 1, window]
                for i in range(local):
                    real = series[side, 1 - kind, 0, start + i]
                    imag = series[side, 1 - kind, 1, start + i]
                    shifted_real, shifted_imag = ahead_real[i : i + local], ahead_imag[i : i + local]
                    sum_real = sum_real + (shifted_real * real + shifted_imag * imag)
                    sum_imag = sum_imag + (shifted_imag * real - shifted_real * imag)
                results += [sum_real, sum_imag]
            return tuple(results)

        zero = jnp.zeros((local, fold, order), f32)
        sums = lax.fori_loop(0, peers - owner, some_energies, (zero,) * 4)
        tiles = []
        for kind in range(2):
            real, imag = sums[2 * kind] * factor, sums[2 * kind + 1] * factor
            top = jnp.where(low_lanes, real, swap(imag))
            bottom = jnp.where(low_lanes, swap(real), imag)
            tiles.append(jnp.concatenate([top, bottom], axis=1).astype(bf16))
        return tiles

    def polar_copy(side, other, slot, kind):
        return pltpu.make_async_remote_copy(
            src_ref=polar_out.at[side, kind, other],
            dst_ref=polar_in.at[side, kind, slot],
            send_sem=polar_send,
            recv_sem=polar_recv.at[side, kind],
            device_id={"energy": other},
            device_id_type=MESH,
        )

    for side in range(2):
        receive_green(side)
        for step in steps:
            other = partner(me, step)
            tiles = correlate(side, other)
            for kind in range(2):
                polar_out[side, kind, other] = tiles[kind]
            for kind in range(2 if side == 0 else 1):
                polar_copy(side, other, me, kind).start()
        if side == 1:
            for step in steps:
                polar_copy(side, partner(me, step), me, 1).start()
        tiles = correlate(side, me)
        for kind in range(2):
            polar_in[side, kind, me] = tiles[kind]

    def out_copy(kind):
        return pltpu.make_async_copy(out_ref.at[kind], out_hbm.at[kind, 0], out_sem.at[kind])

    for kind in range(2):
        for side in range(2):
            arrived = polar_in.at[side, kind, pl.ds(0, peers - 1)]
            pltpu.make_async_copy(arrived, arrived, polar_recv.at[side, kind]).wait()
        lefts = []
        for lag in range(local):
            both = jnp.concatenate(
                [polar_in[side, kind, :, lag].reshape(order, order) for side in range(2)], axis=1
            )
            lefts.append(jnp.dot(coulomb, both, preferred_element_type=f32).astype(bf16))
        screened = lax.dot_general(
            jnp.concatenate(lefts, axis=0),
            spread,
            (((1,), (1,)), ((), ())),
            preferred_element_type=f32,
        ).astype(bf16)
        for lag in range(local):
            rows = screened[lag * order : (lag + 1) * order]
            out_ref[kind, lag, 0] = rows[:, :order]
            out_ref[kind, lag, 1] = rows[:, order:]
        out_copy(kind).start()

    for sent, sem in ((green_out, green_send), (polar_out, polar_send)):
        if sent is green_out:
            part = sent.at[:, pl.ds(0, peers - 1)]
        else:
            part = sent.at[:, :, pl.ds(0, peers - 1)]
        pltpu.make_async_copy(part, part, sem).wait()
    for kind in range(2):
        out_copy(kind).wait()


def fused_body(green_lower, green_diag, green_upper, self_energy, coulomb):
    peers, sites = lax.axis_size("energy"), lax.axis_size("space")
    local, order = green_diag.shape[1], green_diag.shape[-1]
    bf16 = jnp.bfloat16
    share = (2, peers, local, 2, ROWS, order)
    lags = (2, 2, peers, local, ROWS, order)
    series = (2, 2, 2, peers * local + local, ROWS // 2, order)
    dma = pltpu.SemaphoreType.DMA
    return pl.pallas_call(
        functools.partial(fused_kernel, peers, sites),
        out_shape=jax.ShapeDtypeStruct(self_energy.shape, bf16),
        in_specs=[pl.BlockSpec(memory_space=pltpu.HBM)] * 5,
        out_specs=pl.BlockSpec(memory_space=pltpu.HBM),
        scratch_shapes=[
            pltpu.VMEM((local, 3, 2, order, order), bf16),
            pltpu.VMEM((2, local, 2, order, order), bf16),
            pltpu.VMEM((order, order), bf16),
            pltpu.VMEM((2, local, 2, 2, order, order), bf16),
            pltpu.VMEM((local, 2 * order, 2 * order), jnp.float32),
            pltpu.VMEM(share, bf16),
            pltpu.VMEM(share, bf16),
            pltpu.VMEM(series, jnp.float32),
            pltpu.VMEM(lags, bf16),
            pltpu.VMEM(lags, bf16),
            pltpu.VMEM((2, local, 2, order, order), bf16),
            dma((2,)),
            dma((local, 2)),
            dma,
            dma((2, local)),
            dma((2, local)),
            dma,
            dma((2, peers)),
            dma,
            dma((2, 2)),
        ],
        compiler_params=pltpu.CompilerParams(
            collective_id=0, has_side_effects=True, vmem_limit_bytes=64 * 2**20 - 2**15
        ),
    )(green_lower, green_diag, green_upper, self_energy, coulomb)


def body(green_lower, green_diag, green_upper, self_energy, coulomb):
    peers = lax.axis_size("energy")
    blocks, order = green_diag.shape[0], green_diag.shape[-1]
    if blocks == 1 and order == 128 and order == peers * ROWS and peers & (peers - 1) == 0:
        return fused_body(green_lower, green_diag, green_upper, self_energy, coulomb)
    return plain_body(green_lower, green_diag, green_upper, self_energy, coulomb)


def solution(mesh):
    in_specs = (
        P("space", "energy", None, None, None),
        P("space", "energy", None, None, None),
        P("space", "energy", None, None, None),
        P(None, "space", "energy", None, None, None),
        P("space", None, None),
    )
    out_specs = P(None, "space", "energy", None, None, None)
    return jax.shard_map(body, mesh=mesh, in_specs=in_specs, out_specs=out_specs, check_vma=False)
```

```python
import functools
import math

import jax
import jax.numpy as jnp
from jax import lax
from jax.experimental import pallas as pl
from jax.experimental.pallas import tpu as pltpu
from jax.sharding import PartitionSpec as P


def padded_2(shard, sides, width):
    for axis, dim in sides:
        peers, length = (lax.axis_size(axis), shard.shape[dim])
        up = [(i, (i + 1) % peers) for i in range(peers - 1)]
        down = [(j, i) for i, j in up]
        last = lax.slice_in_dim(shard, length - width, length, axis=dim)
        initial = lax.slice_in_dim(shard, 0, width, axis=dim)
        before = lax.ppermute(last, axis, up)
        after = lax.ppermute(initial, axis, down)
        shard = jnp.concatenate([before, shard, after], axis=dim)
    return shard


def congruence(green, sigma):
    green_real = green[:, :, 0]
    green_imag = green[:, :, 1]
    sigma_real = sigma[:, :, :, 0]
    sigma_imag = sigma[:, :, :, 1]
    green_wide = jnp.concatenate([green_real, green_imag], axis=-1)
    sigma_tall = jnp.concatenate(
        [
            jnp.concatenate([sigma_real, sigma_imag], axis=-1),
            jnp.concatenate([-sigma_imag, sigma_real], axis=-1),
        ],
        axis=-2,
    )
    mixed = jnp.einsum(
        "nepq,fneqr->fnepr", green_wide, sigma_tall, preferred_element_type=jnp.float32
    ).astype(jnp.bfloat16)
    adjoint_tall = jnp.concatenate(
        [green_wide, jnp.concatenate([-green_imag, green_real], axis=-1)], axis=-2
    )
    return jnp.einsum("fnepr,nesr->fneps", mixed, adjoint_tall, preferred_element_type=jnp.float32)


def split_table(table):
    high_part = table.astype(jnp.bfloat16)
    low_part = (table - high_part.astype(jnp.float32)).astype(jnp.bfloat16)
    return (high_part, low_part)


def spectrum(values, table_high, table_low, padded_len):

    def apply_table(part):
        return jnp.dot(table_high, part, preferred_element_type=jnp.float32) + jnp.dot(
            table_low, part, preferred_element_type=jnp.float32
        )

    real_terms = apply_table(values[:, 0])
    imag_terms = apply_table(values[:, 1])
    out_real = real_terms[:padded_len] + imag_terms[padded_len:]
    out_imag = imag_terms[:padded_len] - real_terms[padded_len:]
    return (out_real, out_imag)


def plain_body(green_lower, green_diag, green_upper, self_energy, coulomb):
    block_count = green_diag.shape[0]
    energy_local = green_diag.shape[1]
    block_order = green_diag.shape[-1]
    energies = energy_local * lax.axis_size("energy")
    padded_len = 2 * energies
    padded = padded_2(self_energy, (("space", 1),), 1)
    lower_term = congruence(green_lower, padded[:, :block_count])
    diag_term = congruence(green_diag, padded[:, 1 : block_count + 1])
    upper_term = congruence(green_upper, padded[:, 2:])
    total = lower_term + diag_term + upper_term
    total = total.reshape(2, block_count, energy_local, block_order, 2, block_order)
    green_function = (
        jnp.transpose(total, (0, 2, 4, 1, 3, 5))
        .astype(jnp.bfloat16)
        .reshape(2, energy_local, 2, -1)
    )
    frequency = lax.iota(jnp.int32, padded_len)
    energy_index = lax.iota(jnp.int32, energies)
    step_angle = 2.0 * math.pi / padded_len
    forward_angle = (frequency[:, None] * energy_index[None, :] % padded_len).astype(
        jnp.float32
    ) * step_angle
    forward_table = jnp.concatenate([jnp.cos(forward_angle), jnp.sin(forward_angle)], axis=0)
    table_high, table_low = split_table(forward_table)
    lesser_values = lax.all_to_all(
        green_function[0], "energy", split_axis=2, concat_axis=0, tiled=True
    )
    greater_values = lax.all_to_all(
        green_function[1], "energy", split_axis=2, concat_axis=0, tiled=True
    )
    lesser_real, lesser_imag = spectrum(lesser_values, table_high, table_low, padded_len)
    greater_real, greater_imag = spectrum(greater_values, table_high, table_low, padded_len)
    product_real = lesser_real * greater_real + lesser_imag * greater_imag
    product_imag = lesser_imag * greater_real - lesser_real * greater_imag
    row_index = jnp.concatenate([energy_index, (padded_len - energy_index) % padded_len])
    back_angle = (row_index[:, None] * frequency[None, :] % padded_len).astype(
        jnp.float32
    ) * step_angle
    back_cos = jnp.cos(back_angle)
    back_sin = jnp.sin(back_angle)
    back_table = jnp.concatenate(
        [
            jnp.concatenate([back_cos, -back_sin], axis=1),
            jnp.concatenate([back_sin, back_cos], axis=1),
        ],
        axis=0,
    )
    stacked_product = jnp.concatenate([product_real, product_imag], axis=0)
    factor = 1.0 / (padded_len * math.sqrt(energies))
    combined = (
        jnp.dot(
            back_table,
            stacked_product,
            precision=lax.Precision.HIGH,
            preferred_element_type=jnp.float32,
        )
        * factor
    )
    corr_real = combined[:padded_len]
    corr_imag = combined[padded_len:]
    lesser_lags = jnp.stack([corr_real[:energies], corr_imag[:energies]], axis=1)
    greater_lags = jnp.stack([corr_real[energies:], -corr_imag[energies:]], axis=1)
    polar = jnp.stack([lesser_lags, greater_lags], axis=0).astype(jnp.bfloat16)
    returned = lax.all_to_all(polar, "energy", split_axis=1, concat_axis=3, tiled=True)
    returned = returned.reshape(2, energy_local, 2, block_count, block_order, block_order)
    left_product = jnp.einsum(
        "npq,fetnqr->fetnpr", coulomb, returned, preferred_element_type=jnp.float32
    ).astype(jnp.bfloat16)
    screened = jnp.einsum(
        "fetnpr,nsr->fnetps", left_product, coulomb, preferred_element_type=jnp.float32
    )
    return screened.astype(jnp.bfloat16)


ROWS = 16
MESH = pl.DeviceIdType.MESH


def partner(me, step):
    other, bit = me, 1
    while bit <= step:
        if step & bit:
            other = other + bit * (1 - 2 * lax.rem(lax.div(me, bit), 2))
        bit *= 2
    return other


def alternate(peers):
    far, near = list(range(peers // 2, peers)), list(range(1, peers // 2))
    steps = []
    for i in range(peers // 2):
        steps += far[i : i + 1] + near[i : i + 1]
    return steps


def rotation(real, imag):
    return jnp.concatenate(
        [
            jnp.concatenate([real, imag], axis=1),
            jnp.concatenate([-imag, real], axis=1),
        ],
        axis=0,
    )


def fused_kernel(
    peers,
    sites,
    lower_hbm,
    diag_hbm,
    upper_hbm,
    sigma_hbm,
    coulomb_hbm,
    out_ref,
    greens,
    sigma_ref,
    coulomb_ref,
    halo,
    total,
    green_out,
    green_in,
    series,
    polar_out,
    polar_in,
    load_sem,
    coulomb_sem,
    halo_send,
    halo_recv,
    green_send,
    green_recv,
    polar_send,
    polar_recv,
):
    me = lax.axis_index("energy")
    site = lax.axis_index("space")
    has_next = site < sites - 1
    has_previous = site > 0
    next_site = lax.rem(site + 1, sites)
    previous_site = lax.rem(site + sites - 1, sites)
    local, order = greens.shape[0], greens.shape[-1]
    half = order // 2
    energies = peers * local
    steps = alternate(peers)
    f32, bf16 = jnp.float32, jnp.bfloat16

    barrier = pltpu.get_barrier_semaphore()
    for step in steps:
        pl.semaphore_signal(
            barrier, inc=1, device_id={"energy": partner(me, step)}, device_id_type=MESH
        )

    @pl.when(has_next)
    def _():
        pl.semaphore_signal(barrier, inc=1, device_id={"space": next_site}, device_id_type=MESH)

    @pl.when(has_previous)
    def _():
        pl.semaphore_signal(barrier, inc=1, device_id={"space": previous_site}, device_id_type=MESH)

    def load_sigma(energy):
        return pltpu.make_async_copy(
            sigma_hbm.at[:, 0, energy], sigma_ref.at[:, energy], load_sem.at[energy, 0]
        )

    sources = (diag_hbm, lower_hbm, upper_hbm)
    for energy in range(local):
        load_sigma(energy).start()
        for i, source in enumerate(sources):
            pltpu.make_async_copy(
                source.at[0, energy], greens.at[energy, i], load_sem.at[energy, 1]
            ).start()
    coulomb_load = pltpu.make_async_copy(coulomb_hbm.at[0], coulomb_ref, coulomb_sem)
    coulomb_load.start()

    neighbours = jnp.where(has_next, 1, 0) + jnp.where(has_previous, 1, 0)
    pl.semaphore_wait(barrier, peers - 1 + neighbours)

    def halo_copy(side, energy):
        return pltpu.make_async_remote_copy(
            src_ref=sigma_hbm.at[:, 0, energy],
            dst_ref=halo.at[side, energy],
            send_sem=halo_send.at[side, energy],
            recv_sem=halo_recv.at[side, energy],
            device_id={"space": next_site if side == 0 else previous_site},
            device_id_type=MESH,
        )

    def each_halo(energy, act):
        @pl.when(has_next)
        def _():
            act(halo_copy(0, energy))

        @pl.when(has_previous)
        def _():
            act(halo_copy(1, energy))

    for energy in range(min(2, local)):
        each_halo(energy, lambda copy: copy.start())

    @pl.when(jnp.logical_not(has_previous))
    def _():
        halo[0] = jnp.zeros(halo.shape[1:], halo.dtype)

    @pl.when(jnp.logical_not(has_next))
    def _():
        halo[1] = jnp.zeros(halo.shape[1:], halo.dtype)

    early = max(local - 2, 0)

    def green_copy(other, slot, group, energies_sent, sides_sent):
        return pltpu.make_async_remote_copy(
            src_ref=green_out.at[other, energies_sent, sides_sent],
            dst_ref=green_in.at[slot, energies_sent, sides_sent],
            send_sem=green_send,
            recv_sem=green_recv.at[group, slot],
            device_id={"energy": other},
            device_id_type=MESH,
        )

    def send_green(group, first, count, side, sides):
        for step in steps:
            green_copy(
                partner(me, step), me, group, pl.ds(first, count), pl.ds(side, sides)
            ).start()

    def term(energy, terms):
        mixed, adjoint = [], []
        for which, sigma_of in terms:
            real, imag = greens[energy, which, 0], greens[energy, which, 1]
            wide = jnp.concatenate([real, imag], axis=1)
            mixed.append(
                jnp.concatenate(
                    [
                        jnp.dot(
                            wide,
                            rotation(sigma_of(kind, 0), sigma_of(kind, 1)),
                            preferred_element_type=f32,
                        ).astype(bf16)
                        for kind in range(2)
                    ],
                    axis=0,
                )
            )
            adjoint.append(
                jnp.concatenate(
                    [rotation(real[:half], imag[:half]), rotation(real[half:], imag[half:])],
                    axis=0,
                )
            )
        return lax.dot_general(
            jnp.concatenate(mixed, axis=1),
            jnp.concatenate(adjoint, axis=1),
            (((1,), (1,)), ((), ())),
            preferred_element_type=f32,
        )

    def own_term(energy):
        load_sigma(energy).wait()
        pltpu.make_async_copy(greens.at[energy], greens.at[energy], load_sem.at[energy, 1]).wait()
        total[energy] = term(energy, [(0, lambda kind, part: sigma_ref[kind, energy, part])])

    for energy in range(min(2, local)):
        own_term(energy)
    for energy in range(local):

        @pl.when(has_previous)
        def _():
            halo_copy(0, energy).wait_recv()

        @pl.when(has_next)
        def _():
            halo_copy(1, energy).wait_recv()

        each_halo(energy, lambda copy: copy.wait_send())
        if energy + 2 < local:
            each_halo(energy + 2, lambda copy: copy.start())
        coupled = term(
            energy,
            [
                (1, lambda kind, part: halo[0, energy, kind, part]),
                (2, lambda kind, part: halo[1, energy, kind, part]),
            ],
        )
        rounded = (total[energy] + coupled).astype(bf16)
        for side in range(2):
            for kind in range(2):
                block = rounded[
                    kind * order : (kind + 1) * order, side * order : (side + 1) * order
                ]
                green_out[:, energy, side, kind] = block.reshape(peers, ROWS, order)
        if energy < early:
            send_green(0, energy, 1, 0, 2)
        elif energy == local - 1:
            for side in range(2):
                send_green(side, early, local - early, side, 1)
        if energy + 2 < local:
            own_term(energy + 2)

    coulomb_load.wait()
    coulomb = coulomb_ref[...]
    in_low = lax.broadcasted_iota(jnp.int32, (order, order), 1) < half
    straight = coulomb.astype(f32)
    swapped = pltpu.roll(straight, half, 1)
    zeros = jnp.zeros_like(straight)
    spread = jnp.concatenate(
        [
            jnp.concatenate(
                [jnp.where(in_low, straight, zeros), jnp.where(in_low, swapped, zeros)], axis=1
            ),
            jnp.concatenate(
                [jnp.where(in_low, zeros, swapped), jnp.where(in_low, zeros, straight)], axis=1
            ),
        ],
        axis=0,
    ).astype(bf16)

    fold = ROWS // 2
    low_lanes = lax.broadcasted_iota(jnp.int32, (local, fold, order), 2) < half

    def swap(values):
        return pltpu.roll(values.reshape(-1, order), half, 1).reshape(values.shape)

    tail = series.shape[3] - energies
    for side in range(2):
        for kind in range(2):
            for part in range(2):
                series[side, kind, part, energies:] = jnp.zeros((tail, fold, order), f32)

    def unpack(side, source, values):
        for kind in range(2):
            tile = values[:, kind].astype(f32)
            top, bottom = tile[:, :fold], tile[:, fold:]
            where = pl.ds(source * local, local)
            series[side, kind, 0, where] = jnp.where(low_lanes, top, swap(bottom))
            series[side, kind, 1, where] = jnp.where(low_lanes, swap(top), bottom)

    def units_of(ref, slot, units):
        if units % 2 == 0:
            return ref.at[slot, pl.ds(0, units // 2)]
        return ref.at[slot, pl.ds(0, units), 0]

    def receive_green(side):
        unpack(side, me, green_out[me, :, side])
        for step in steps:
            other = partner(me, step)
            units = 2 * early * (1 - side) + local - early
            arrived = units_of(green_in, other, units)
            pltpu.make_async_copy(arrived, arrived, green_recv.at[side, other]).wait()
            unpack(side, other, green_in[other, :, side])

    factor = 1.0 / math.sqrt(energies)

    def correlate(side, owner):
        first_lag = owner * local

        def some_energies(index, sums):
            start = index * local
            window = pl.ds(start + first_lag, 2 * local - 1)
            results = []
            for kind in range(2):
                sum_real, sum_imag = sums[2 * kind : 2 * kind + 2]
                ahead_real, ahead_imag = series[side, kind, 0, window], series[side, kind, 1, window]
                for i in range(local):
                    real = series[side, 1 - kind, 0, start + i]
                    imag = series[side, 1 - kind, 1, start + i]
                    shifted_real, shifted_imag = ahead_real[i : i + local], ahead_imag[i : i + local]
                    sum_real = sum_real + (shifted_real * real + shifted_imag * imag)
                    sum_imag = sum_imag + (shifted_imag * real - shifted_real * imag)
                results += [sum_real, sum_imag]
            return tuple(results)

        zero = jnp.zeros((local, fold, order), f32)
        sums = lax.fori_loop(0, peers - owner, some_energies, (zero,) * 4)
        tiles = []
        for kind in range(2):
            real, imag = sums[2 * kind] * factor, sums[2 * kind + 1] * factor
            top = jnp.where(low_lanes, real, swap(imag))
            bottom = jnp.where(low_lanes, swap(real), imag)
            tiles.append(jnp.concatenate([top, bottom], axis=1).astype(bf16))
        return tiles

    def polar_copy(other, slot, kind):
        where = (0,) if kind is None else (1, kind)
        return pltpu.make_async_remote_copy(
            src_ref=polar_out.at[where[0], other, *where[1:]],
            dst_ref=polar_in.at[where[0], slot, *where[1:]],
            send_sem=polar_send,
            recv_sem=polar_recv.at[0 if kind is None else 1 + kind],
            device_id={"energy": other},
            device_id_type=MESH,
        )

    for side in range(2):
        receive_green(side)
        for step in steps:
            other = partner(me, step)
            tiles = correlate(side, other)
            for kind in range(2):
                polar_out[side, other, kind] = tiles[kind]
            polar_copy(other, me, None if side == 0 else 0).start()
        if side == 1:
            for step in steps:
                polar_copy(partner(me, step), me, 1).start()
        tiles = correlate(side, me)
        for kind in range(2):
            polar_in[side, me, kind] = tiles[kind]

    for kind in range(2):
        if kind == 0:
            arrived = polar_in.at[0, pl.ds(0, peers - 1)]
            pltpu.make_async_copy(arrived, arrived, polar_recv.at[0]).wait()
        arrived = polar_in.at[1, pl.ds(0, peers - 1), kind]
        pltpu.make_async_copy(arrived, arrived, polar_recv.at[1 + kind]).wait()
        lefts = []
        for lag in range(local):
            both = jnp.concatenate(
                [polar_in[side, :, kind, lag].reshape(order, order) for side in range(2)], axis=1
            )
            lefts.append(jnp.dot(coulomb, both, preferred_element_type=f32).astype(bf16))
        screened = lax.dot_general(
            jnp.concatenate(lefts, axis=0),
            spread,
            (((1,), (1,)), ((), ())),
            preferred_element_type=f32,
        ).astype(bf16)
        for lag in range(local):
            rows = screened[lag * order : (lag + 1) * order]
            out_ref[kind, 0, lag, 0] = rows[:, :order]
            out_ref[kind, 0, lag, 1] = rows[:, order:]

    part = green_out.at[pl.ds(0, peers - 1)]
    pltpu.make_async_copy(part, part, green_send).wait()
    part = polar_out.at[:, pl.ds(0, peers - 1)]
    pltpu.make_async_copy(part, part, polar_send).wait()


def fused_body(green_lower, green_diag, green_upper, self_energy, coulomb):
    peers, sites = lax.axis_size("energy"), lax.axis_size("space")
    local, order = green_diag.shape[1], green_diag.shape[-1]
    bf16 = jnp.bfloat16
    share = (peers, local, 2, 2, ROWS, order)
    lags = (2, peers, 2, local, ROWS, order)
    series = (2, 2, 2, peers * local + local, ROWS // 2, order)
    dma = pltpu.SemaphoreType.DMA
    room = 64 * 2**20 - 2 * self_energy.size - 2**17
    return pl.pallas_call(
        functools.partial(fused_kernel, peers, sites),
        out_shape=pltpu.VMEM(self_energy.shape, bf16),
        in_specs=[pl.BlockSpec(memory_space=pltpu.HBM)] * 5,
        out_specs=pl.BlockSpec(memory_space=pltpu.VMEM),
        scratch_shapes=[
            pltpu.VMEM((local, 3, 2, order, order), bf16),
            pltpu.VMEM((2, local, 2, order, order), bf16),
            pltpu.VMEM((order, order), bf16),
            pltpu.VMEM((2, local, 2, 2, order, order), bf16),
            pltpu.VMEM((local, 2 * order, 2 * order), jnp.float32),
            pltpu.VMEM(share, bf16),
            pltpu.VMEM(share, bf16),
            pltpu.VMEM(series, jnp.float32),
            pltpu.VMEM(lags, bf16),
            pltpu.VMEM(lags, bf16),
            dma((local, 2)),
            dma,
            dma((2, local)),
            dma((2, local)),
            dma,
            dma((2, peers)),
            dma,
            dma((3,)),
        ],
        compiler_params=pltpu.CompilerParams(
            collective_id=0, has_side_effects=True, vmem_limit_bytes=room
        ),
    )(green_lower, green_diag, green_upper, self_energy, coulomb)


def body(green_lower, green_diag, green_upper, self_energy, coulomb):
    peers = lax.axis_size("energy")
    blocks, order = green_diag.shape[0], green_diag.shape[-1]
    if blocks == 1 and order == 128 and order == peers * ROWS and peers & (peers - 1) == 0:
        return fused_body(green_lower, green_diag, green_upper, self_energy, coulomb)
    return plain_body(green_lower, green_diag, green_upper, self_energy, coulomb)


def solution(mesh):
    in_specs = (
        P("space", "energy", None, None, None),
        P("space", "energy", None, None, None),
        P("space", "energy", None, None, None),
        P(None, "space", "energy", None, None, None),
        P("space", None, None),
    )
    out_specs = P(None, "space", "energy", None, None, None)
    return jax.shard_map(body, mesh=mesh, in_specs=in_specs, out_specs=out_specs, check_vma=False)
```

```python
import functools
import math

import jax
import jax.numpy as jnp
from jax import lax
from jax.experimental import pallas as pl
from jax.experimental.pallas import tpu as pltpu
from jax.sharding import PartitionSpec as P


def padded_2(shard, sides, width):
    for axis, dim in sides:
        peers, length = (lax.axis_size(axis), shard.shape[dim])
        up = [(i, (i + 1) % peers) for i in range(peers - 1)]
        down = [(j, i) for i, j in up]
        last = lax.slice_in_dim(shard, length - width, length, axis=dim)
        initial = lax.slice_in_dim(shard, 0, width, axis=dim)
        before = lax.ppermute(last, axis, up)
        after = lax.ppermute(initial, axis, down)
        shard = jnp.concatenate([before, shard, after], axis=dim)
    return shard


def congruence(green, sigma):
    green_real = green[:, :, 0]
    green_imag = green[:, :, 1]
    sigma_real = sigma[:, :, :, 0]
    sigma_imag = sigma[:, :, :, 1]
    green_wide = jnp.concatenate([green_real, green_imag], axis=-1)
    sigma_tall = jnp.concatenate(
        [
            jnp.concatenate([sigma_real, sigma_imag], axis=-1),
            jnp.concatenate([-sigma_imag, sigma_real], axis=-1),
        ],
        axis=-2,
    )
    mixed = jnp.einsum(
        "nepq,fneqr->fnepr", green_wide, sigma_tall, preferred_element_type=jnp.float32
    ).astype(jnp.bfloat16)
    adjoint_tall = jnp.concatenate(
        [green_wide, jnp.concatenate([-green_imag, green_real], axis=-1)], axis=-2
    )
    return jnp.einsum("fnepr,nesr->fneps", mixed, adjoint_tall, preferred_element_type=jnp.float32)


def split_table(table):
    high_part = table.astype(jnp.bfloat16)
    low_part = (table - high_part.astype(jnp.float32)).astype(jnp.bfloat16)
    return (high_part, low_part)


def spectrum(values, table_high, table_low, padded_len):

    def apply_table(part):
        return jnp.dot(table_high, part, preferred_element_type=jnp.float32) + jnp.dot(
            table_low, part, preferred_element_type=jnp.float32
        )

    real_terms = apply_table(values[:, 0])
    imag_terms = apply_table(values[:, 1])
    out_real = real_terms[:padded_len] + imag_terms[padded_len:]
    out_imag = imag_terms[:padded_len] - real_terms[padded_len:]
    return (out_real, out_imag)


def plain_body(green_lower, green_diag, green_upper, self_energy, coulomb):
    block_count = green_diag.shape[0]
    energy_local = green_diag.shape[1]
    block_order = green_diag.shape[-1]
    energies = energy_local * lax.axis_size("energy")
    padded_len = 2 * energies
    padded = padded_2(self_energy, (("space", 1),), 1)
    lower_term = congruence(green_lower, padded[:, :block_count])
    diag_term = congruence(green_diag, padded[:, 1 : block_count + 1])
    upper_term = congruence(green_upper, padded[:, 2:])
    total = lower_term + diag_term + upper_term
    total = total.reshape(2, block_count, energy_local, block_order, 2, block_order)
    green_function = (
        jnp.transpose(total, (0, 2, 4, 1, 3, 5))
        .astype(jnp.bfloat16)
        .reshape(2, energy_local, 2, -1)
    )
    frequency = lax.iota(jnp.int32, padded_len)
    energy_index = lax.iota(jnp.int32, energies)
    step_angle = 2.0 * math.pi / padded_len
    forward_angle = (frequency[:, None] * energy_index[None, :] % padded_len).astype(
        jnp.float32
    ) * step_angle
    forward_table = jnp.concatenate([jnp.cos(forward_angle), jnp.sin(forward_angle)], axis=0)
    table_high, table_low = split_table(forward_table)
    lesser_values = lax.all_to_all(
        green_function[0], "energy", split_axis=2, concat_axis=0, tiled=True
    )
    greater_values = lax.all_to_all(
        green_function[1], "energy", split_axis=2, concat_axis=0, tiled=True
    )
    lesser_real, lesser_imag = spectrum(lesser_values, table_high, table_low, padded_len)
    greater_real, greater_imag = spectrum(greater_values, table_high, table_low, padded_len)
    product_real = lesser_real * greater_real + lesser_imag * greater_imag
    product_imag = lesser_imag * greater_real - lesser_real * greater_imag
    row_index = jnp.concatenate([energy_index, (padded_len - energy_index) % padded_len])
    back_angle = (row_index[:, None] * frequency[None, :] % padded_len).astype(
        jnp.float32
    ) * step_angle
    back_cos = jnp.cos(back_angle)
    back_sin = jnp.sin(back_angle)
    back_table = jnp.concatenate(
        [
            jnp.concatenate([back_cos, -back_sin], axis=1),
            jnp.concatenate([back_sin, back_cos], axis=1),
        ],
        axis=0,
    )
    stacked_product = jnp.concatenate([product_real, product_imag], axis=0)
    factor = 1.0 / (padded_len * math.sqrt(energies))
    combined = (
        jnp.dot(
            back_table,
            stacked_product,
            precision=lax.Precision.HIGH,
            preferred_element_type=jnp.float32,
        )
        * factor
    )
    corr_real = combined[:padded_len]
    corr_imag = combined[padded_len:]
    lesser_lags = jnp.stack([corr_real[:energies], corr_imag[:energies]], axis=1)
    greater_lags = jnp.stack([corr_real[energies:], -corr_imag[energies:]], axis=1)
    polar = jnp.stack([lesser_lags, greater_lags], axis=0).astype(jnp.bfloat16)
    returned = lax.all_to_all(polar, "energy", split_axis=1, concat_axis=3, tiled=True)
    returned = returned.reshape(2, energy_local, 2, block_count, block_order, block_order)
    left_product = jnp.einsum(
        "npq,fetnqr->fetnpr", coulomb, returned, preferred_element_type=jnp.float32
    ).astype(jnp.bfloat16)
    screened = jnp.einsum(
        "fetnpr,nsr->fnetps", left_product, coulomb, preferred_element_type=jnp.float32
    )
    return screened.astype(jnp.bfloat16)


ROWS = 16
MESH = pl.DeviceIdType.MESH


def partner(me, step):
    other, bit = me, 1
    while bit <= step:
        if step & bit:
            other = other + bit * (1 - 2 * lax.rem(lax.div(me, bit), 2))
        bit *= 2
    return other


def alternate(peers):
    far, near = list(range(peers // 2, peers)), list(range(1, peers // 2))
    steps = []
    for i in range(peers // 2):
        steps += far[i : i + 1] + near[i : i + 1]
    return steps


def rotation(real, imag):
    return jnp.concatenate(
        [
            jnp.concatenate([real, imag], axis=1),
            jnp.concatenate([-imag, real], axis=1),
        ],
        axis=0,
    )


def fused_kernel(
    peers,
    sites,
    lower_hbm,
    diag_hbm,
    upper_hbm,
    sigma_hbm,
    coulomb_hbm,
    out_ref,
    greens,
    sigma_ref,
    coulomb_ref,
    halo,
    green_out,
    green_in,
    series,
    polar_out,
    polar_in,
    load_sem,
    coulomb_sem,
    halo_send,
    halo_recv,
    green_send,
    green_recv,
    polar_send,
    polar_recv,
):
    me = lax.axis_index("energy")
    site = lax.axis_index("space")
    has_next = site < sites - 1
    has_previous = site > 0
    next_site = lax.rem(site + 1, sites)
    previous_site = lax.rem(site + sites - 1, sites)
    local, order = greens.shape[0], greens.shape[-1]
    half = order // 2
    energies = peers * local
    steps = alternate(peers)
    f32, bf16 = jnp.float32, jnp.bfloat16

    barrier = pltpu.get_barrier_semaphore()
    for step in steps:
        pl.semaphore_signal(
            barrier, inc=1, device_id={"energy": partner(me, step)}, device_id_type=MESH
        )

    @pl.when(has_next)
    def _():
        pl.semaphore_signal(barrier, inc=1, device_id={"space": next_site}, device_id_type=MESH)

    @pl.when(has_previous)
    def _():
        pl.semaphore_signal(barrier, inc=1, device_id={"space": previous_site}, device_id_type=MESH)

    def load_sigma(energy):
        return pltpu.make_async_copy(
            sigma_hbm.at[:, 0, energy], sigma_ref.at[:, energy], load_sem.at[energy, 0]
        )

    sources = (diag_hbm, lower_hbm, upper_hbm)
    for energy in range(local):
        load_sigma(energy).start()
        for i, source in enumerate(sources):
            pltpu.make_async_copy(
                source.at[0, energy], greens.at[energy, i], load_sem.at[energy, 1]
            ).start()
    coulomb_load = pltpu.make_async_copy(coulomb_hbm.at[0], coulomb_ref, coulomb_sem)
    coulomb_load.start()

    neighbours = jnp.where(has_next, 1, 0) + jnp.where(has_previous, 1, 0)
    pl.semaphore_wait(barrier, peers - 1 + neighbours)

    def halo_copy(side, energy):
        return pltpu.make_async_remote_copy(
            src_ref=sigma_hbm.at[:, 0, energy],
            dst_ref=halo.at[side, energy],
            send_sem=halo_send.at[side, energy],
            recv_sem=halo_recv.at[side, energy],
            device_id={"space": next_site if side == 0 else previous_site},
            device_id_type=MESH,
        )

    def each_halo(energy, act):
        @pl.when(has_next)
        def _():
            act(halo_copy(0, energy))

        @pl.when(has_previous)
        def _():
            act(halo_copy(1, energy))

    each_halo(0, lambda copy: copy.start())

    @pl.when(jnp.logical_not(has_previous))
    def _():
        halo[0] = jnp.zeros(halo.shape[1:], halo.dtype)

    @pl.when(jnp.logical_not(has_next))
    def _():
        halo[1] = jnp.zeros(halo.shape[1:], halo.dtype)

    early = max(local - 2, 0)

    def green_copy(other, slot, group, energies_sent, sides_sent):
        return pltpu.make_async_remote_copy(
            src_ref=green_out.at[other, energies_sent, sides_sent],
            dst_ref=green_in.at[slot, energies_sent, sides_sent],
            send_sem=green_send,
            recv_sem=green_recv.at[group, slot],
            device_id={"energy": other},
            device_id_type=MESH,
        )

    def send_green(group, first, count, side, sides):
        for step in steps:
            green_copy(
                partner(me, step), me, group, pl.ds(first, count), pl.ds(side, sides)
            ).start()

    def term(energy, terms):
        mixed, adjoint = [], []
        for which, sigma_of in terms:
            real, imag = greens[energy, which, 0], greens[energy, which, 1]
            wide = jnp.concatenate([real, imag], axis=1)
            mixed.append(
                jnp.concatenate(
                    [
                        jnp.dot(
                            wide,
                            rotation(sigma_of(kind, 0), sigma_of(kind, 1)),
                            preferred_element_type=f32,
                        ).astype(bf16)
                        for kind in range(2)
                    ],
                    axis=0,
                )
            )
            adjoint.append(
                jnp.concatenate(
                    [rotation(real[:half], imag[:half]), rotation(real[half:], imag[half:])],
                    axis=0,
                )
            )
        return lax.dot_general(
            jnp.concatenate(mixed, axis=1),
            jnp.concatenate(adjoint, axis=1),
            (((1,), (1,)), ((), ())),
            preferred_element_type=f32,
        )

    def own_term(energy):
        load_sigma(energy).wait()
        pltpu.make_async_copy(greens.at[energy], greens.at[energy], load_sem.at[energy, 1]).wait()
        return term(energy, [(0, lambda kind, part: sigma_ref[kind, energy, part])])

    for energy in range(local):
        total = own_term(energy)
        if energy + 1 < local:
            each_halo(energy + 1, lambda copy: copy.start())

        @pl.when(has_previous)
        def _():
            halo_copy(0, energy).wait_recv()

        @pl.when(has_next)
        def _():
            halo_copy(1, energy).wait_recv()

        each_halo(energy, lambda copy: copy.wait_send())
        coupled = term(
            energy,
            [
                (1, lambda kind, part: halo[0, energy, kind, part]),
                (2, lambda kind, part: halo[1, energy, kind, part]),
            ],
        )
        rounded = (total + coupled).astype(bf16)
        for side in range(2):
            for kind in range(2):
                block = rounded[
                    kind * order : (kind + 1) * order, side * order : (side + 1) * order
                ]
                green_out[:, energy, side, kind] = block.reshape(peers, ROWS, order)
        if energy < early:
            send_green(0, energy, 1, 0, 2)
        elif energy == local - 1:
            for side in range(2):
                send_green(side, early, local - early, side, 1)

    coulomb_load.wait()
    coulomb = coulomb_ref[...]
    in_low = lax.broadcasted_iota(jnp.int32, (order, order), 1) < half
    straight = coulomb.astype(f32)
    swapped = pltpu.roll(straight, half, 1)
    zeros = jnp.zeros_like(straight)
    spread = jnp.concatenate(
        [
            jnp.concatenate(
                [jnp.where(in_low, straight, zeros), jnp.where(in_low, swapped, zeros)], axis=1
            ),
            jnp.concatenate(
                [jnp.where(in_low, zeros, swapped), jnp.where(in_low, zeros, straight)], axis=1
            ),
        ],
        axis=0,
    ).astype(bf16)

    fold = ROWS // 2
    low_lanes = lax.broadcasted_iota(jnp.int32, (local, fold, order), 2) < half

    def swap(values):
        return pltpu.roll(values.reshape(-1, order), half, 1).reshape(values.shape)

    tail = series.shape[3] - energies
    for side in range(2):
        for kind in range(2):
            for part in range(2):
                series[side, kind, part, energies:] = jnp.zeros((tail, fold, order), f32)

    def unpack(side, source, values):
        for kind in range(2):
            tile = values[:, kind].astype(f32)
            top, bottom = tile[:, :fold], tile[:, fold:]
            where = pl.ds(source * local, local)
            series[side, kind, 0, where] = jnp.where(low_lanes, top, swap(bottom))
            series[side, kind, 1, where] = jnp.where(low_lanes, swap(top), bottom)

    def units_of(ref, slot, units):
        if units % 2 == 0:
            return ref.at[slot, pl.ds(0, units // 2)]
        return ref.at[slot, pl.ds(0, units), 0]

    def receive_green(side):
        unpack(side, me, green_out[me, :, side])
        for step in steps:
            other = partner(me, step)
            units = 2 * early * (1 - side) + local - early
            arrived = units_of(green_in, other, units)
            pltpu.make_async_copy(arrived, arrived, green_recv.at[side, other]).wait()
            unpack(side, other, green_in[other, :, side])

    factor = 1.0 / math.sqrt(energies)

    def correlate(side, owner):
        first_lag = owner * local

        def some_energies(index, sums):
            start = index * local
            window = pl.ds(start + first_lag, 2 * local - 1)
            results = []
            for kind in range(2):
                sum_real, sum_imag = sums[2 * kind : 2 * kind + 2]
                ahead_real, ahead_imag = series[side, kind, 0, window], series[side, kind, 1, window]
                for i in range(local):
                    real = series[side, 1 - kind, 0, start + i]
                    imag = series[side, 1 - kind, 1, start + i]
                    shifted_real, shifted_imag = ahead_real[i : i + local], ahead_imag[i : i + local]
                    sum_real = sum_real + (shifted_real * real + shifted_imag * imag)
                    sum_imag = sum_imag + (shifted_imag * real - shifted_real * imag)
                results += [sum_real, sum_imag]
            return tuple(results)

        zero = jnp.zeros((local, fold, order), f32)
        sums = lax.fori_loop(0, peers - owner, some_energies, (zero,) * 4)
        tiles = []
        for kind in range(2):
            real, imag = sums[2 * kind] * factor, sums[2 * kind + 1] * factor
            top = jnp.where(low_lanes, real, swap(imag))
            bottom = jnp.where(low_lanes, swap(real), imag)
            tiles.append(jnp.concatenate([top, bottom], axis=1).astype(bf16))
        return tiles

    def polar_copy(other, slot, kind):
        where = (0,) if kind is None else (1, kind)
        return pltpu.make_async_remote_copy(
            src_ref=polar_out.at[where[0], other, *where[1:]],
            dst_ref=polar_in.at[where[0], slot, *where[1:]],
            send_sem=polar_send,
            recv_sem=polar_recv.at[0 if kind is None else 1 + kind],
            device_id={"energy": other},
            device_id_type=MESH,
        )

    for side in range(2):
        receive_green(side)
        for step in steps:
            other = partner(me, step)
            tiles = correlate(side, other)
            for kind in range(2):
                polar_out[side, other, kind] = tiles[kind]
            polar_copy(other, me, None if side == 0 else 0).start()
        if side == 1:
            for step in steps:
                polar_copy(partner(me, step), me, 1).start()
        tiles = correlate(side, me)
        for kind in range(2):
            polar_in[side, me, kind] = tiles[kind]

    for kind in range(2):
        if kind == 0:
            arrived = polar_in.at[0, pl.ds(0, peers - 1)]
            pltpu.make_async_copy(arrived, arrived, polar_recv.at[0]).wait()
        arrived = polar_in.at[1, pl.ds(0, peers - 1), kind]
        pltpu.make_async_copy(arrived, arrived, polar_recv.at[1 + kind]).wait()
        lefts = []
        for lag in range(local):
            both = jnp.concatenate(
                [polar_in[side, :, kind, lag].reshape(order, order) for side in range(2)], axis=1
            )
            lefts.append(jnp.dot(coulomb, both, preferred_element_type=f32).astype(bf16))
        screened = lax.dot_general(
            jnp.concatenate(lefts, axis=0),
            spread,
            (((1,), (1,)), ((), ())),
            preferred_element_type=f32,
        ).astype(bf16)
        for lag in range(local):
            rows = screened[lag * order : (lag + 1) * order]
            out_ref[kind, 0, lag, 0] = rows[:, :order]
            out_ref[kind, 0, lag, 1] = rows[:, order:]

    part = green_out.at[pl.ds(0, peers - 1)]
    pltpu.make_async_copy(part, part, green_send).wait()
    part = polar_out.at[:, pl.ds(0, peers - 1)]
    pltpu.make_async_copy(part, part, polar_send).wait()


def fused_body(green_lower, green_diag, green_upper, self_energy, coulomb):
    peers, sites = lax.axis_size("energy"), lax.axis_size("space")
    local, order = green_diag.shape[1], green_diag.shape[-1]
    bf16 = jnp.bfloat16
    share = (peers, local, 2, 2, ROWS, order)
    lags = (2, peers, 2, local, ROWS, order)
    series = (2, 2, 2, peers * local + local, ROWS // 2, order)
    dma = pltpu.SemaphoreType.DMA
    room = 64 * 2**20 - 2 * self_energy.size - 2**17
    return pl.pallas_call(
        functools.partial(fused_kernel, peers, sites),
        out_shape=pltpu.VMEM(self_energy.shape, bf16),
        in_specs=[pl.BlockSpec(memory_space=pltpu.HBM)] * 5,
        out_specs=pl.BlockSpec(memory_space=pltpu.VMEM),
        scratch_shapes=[
            pltpu.VMEM((local, 3, 2, order, order), bf16),
            pltpu.VMEM((2, local, 2, order, order), bf16),
            pltpu.VMEM((order, order), bf16),
            pltpu.VMEM((2, local, 2, 2, order, order), bf16),
            pltpu.VMEM(share, bf16),
            pltpu.VMEM(share, bf16),
            pltpu.VMEM(series, jnp.float32),
            pltpu.VMEM(lags, bf16),
            pltpu.VMEM(lags, bf16),
            dma((local, 2)),
            dma,
            dma((2, local)),
            dma((2, local)),
            dma,
            dma((2, peers)),
            dma,
            dma((3,)),
        ],
        compiler_params=pltpu.CompilerParams(
            collective_id=0, has_side_effects=True, vmem_limit_bytes=room
        ),
    )(green_lower, green_diag, green_upper, self_energy, coulomb)


def body(green_lower, green_diag, green_upper, self_energy, coulomb):
    peers = lax.axis_size("energy")
    blocks, order = green_diag.shape[0], green_diag.shape[-1]
    if blocks == 1 and order == 128 and order == peers * ROWS and peers & (peers - 1) == 0:
        return fused_body(green_lower, green_diag, green_upper, self_energy, coulomb)
    return plain_body(green_lower, green_diag, green_upper, self_energy, coulomb)


def solution(mesh):
    in_specs = (
        P("space", "energy", None, None, None),
        P("space", "energy", None, None, None),
        P("space", "energy", None, None, None),
        P(None, "space", "energy", None, None, None),
        P("space", None, None),
    )
    out_specs = P(None, "space", "energy", None, None, None)
    return jax.shard_map(body, mesh=mesh, in_specs=in_specs, out_specs=out_specs, check_vma=False)
```

```python
import functools
import math

import jax
import jax.numpy as jnp
from jax import lax
from jax.experimental import pallas as pl
from jax.experimental.pallas import tpu as pltpu
from jax.sharding import PartitionSpec as P


def padded_2(shard, sides, width):
    for axis, dim in sides:
        peers, length = (lax.axis_size(axis), shard.shape[dim])
        up = [(i, (i + 1) % peers) for i in range(peers - 1)]
        down = [(j, i) for i, j in up]
        last = lax.slice_in_dim(shard, length - width, length, axis=dim)
        initial = lax.slice_in_dim(shard, 0, width, axis=dim)
        before = lax.ppermute(last, axis, up)
        after = lax.ppermute(initial, axis, down)
        shard = jnp.concatenate([before, shard, after], axis=dim)
    return shard


def congruence(green, sigma):
    green_real = green[:, :, 0]
    green_imag = green[:, :, 1]
    sigma_real = sigma[:, :, :, 0]
    sigma_imag = sigma[:, :, :, 1]
    green_wide = jnp.concatenate([green_real, green_imag], axis=-1)
    sigma_tall = jnp.concatenate(
        [
            jnp.concatenate([sigma_real, sigma_imag], axis=-1),
            jnp.concatenate([-sigma_imag, sigma_real], axis=-1),
        ],
        axis=-2,
    )
    mixed = jnp.einsum(
        "nepq,fneqr->fnepr", green_wide, sigma_tall, preferred_element_type=jnp.float32
    ).astype(jnp.bfloat16)
    adjoint_tall = jnp.concatenate(
        [green_wide, jnp.concatenate([-green_imag, green_real], axis=-1)], axis=-2
    )
    return jnp.einsum("fnepr,nesr->fneps", mixed, adjoint_tall, preferred_element_type=jnp.float32)


def split_table(table):
    high_part = table.astype(jnp.bfloat16)
    low_part = (table - high_part.astype(jnp.float32)).astype(jnp.bfloat16)
    return (high_part, low_part)


def spectrum(values, table_high, table_low, padded_len):

    def apply_table(part):
        return jnp.dot(table_high, part, preferred_element_type=jnp.float32) + jnp.dot(
            table_low, part, preferred_element_type=jnp.float32
        )

    real_terms = apply_table(values[:, 0])
    imag_terms = apply_table(values[:, 1])
    out_real = real_terms[:padded_len] + imag_terms[padded_len:]
    out_imag = imag_terms[:padded_len] - real_terms[padded_len:]
    return (out_real, out_imag)


def plain_body(green_lower, green_diag, green_upper, self_energy, coulomb):
    block_count = green_diag.shape[0]
    energy_local = green_diag.shape[1]
    block_order = green_diag.shape[-1]
    energies = energy_local * lax.axis_size("energy")
    padded_len = 2 * energies
    padded = padded_2(self_energy, (("space", 1),), 1)
    lower_term = congruence(green_lower, padded[:, :block_count])
    diag_term = congruence(green_diag, padded[:, 1 : block_count + 1])
    upper_term = congruence(green_upper, padded[:, 2:])
    total = lower_term + diag_term + upper_term
    total = total.reshape(2, block_count, energy_local, block_order, 2, block_order)
    green_function = (
        jnp.transpose(total, (0, 2, 4, 1, 3, 5))
        .astype(jnp.bfloat16)
        .reshape(2, energy_local, 2, -1)
    )
    frequency = lax.iota(jnp.int32, padded_len)
    energy_index = lax.iota(jnp.int32, energies)
    step_angle = 2.0 * math.pi / padded_len
    forward_angle = (frequency[:, None] * energy_index[None, :] % padded_len).astype(
        jnp.float32
    ) * step_angle
    forward_table = jnp.concatenate([jnp.cos(forward_angle), jnp.sin(forward_angle)], axis=0)
    table_high, table_low = split_table(forward_table)
    lesser_values = lax.all_to_all(
        green_function[0], "energy", split_axis=2, concat_axis=0, tiled=True
    )
    greater_values = lax.all_to_all(
        green_function[1], "energy", split_axis=2, concat_axis=0, tiled=True
    )
    lesser_real, lesser_imag = spectrum(lesser_values, table_high, table_low, padded_len)
    greater_real, greater_imag = spectrum(greater_values, table_high, table_low, padded_len)
    product_real = lesser_real * greater_real + lesser_imag * greater_imag
    product_imag = lesser_imag * greater_real - lesser_real * greater_imag
    row_index = jnp.concatenate([energy_index, (padded_len - energy_index) % padded_len])
    back_angle = (row_index[:, None] * frequency[None, :] % padded_len).astype(
        jnp.float32
    ) * step_angle
    back_cos = jnp.cos(back_angle)
    back_sin = jnp.sin(back_angle)
    back_table = jnp.concatenate(
        [
            jnp.concatenate([back_cos, -back_sin], axis=1),
            jnp.concatenate([back_sin, back_cos], axis=1),
        ],
        axis=0,
    )
    stacked_product = jnp.concatenate([product_real, product_imag], axis=0)
    factor = 1.0 / (padded_len * math.sqrt(energies))
    combined = (
        jnp.dot(
            back_table,
            stacked_product,
            precision=lax.Precision.HIGH,
            preferred_element_type=jnp.float32,
        )
        * factor
    )
    corr_real = combined[:padded_len]
    corr_imag = combined[padded_len:]
    lesser_lags = jnp.stack([corr_real[:energies], corr_imag[:energies]], axis=1)
    greater_lags = jnp.stack([corr_real[energies:], -corr_imag[energies:]], axis=1)
    polar = jnp.stack([lesser_lags, greater_lags], axis=0).astype(jnp.bfloat16)
    returned = lax.all_to_all(polar, "energy", split_axis=1, concat_axis=3, tiled=True)
    returned = returned.reshape(2, energy_local, 2, block_count, block_order, block_order)
    left_product = jnp.einsum(
        "npq,fetnqr->fetnpr", coulomb, returned, preferred_element_type=jnp.float32
    ).astype(jnp.bfloat16)
    screened = jnp.einsum(
        "fetnpr,nsr->fnetps", left_product, coulomb, preferred_element_type=jnp.float32
    )
    return screened.astype(jnp.bfloat16)


ROWS = 16
MESH = pl.DeviceIdType.MESH


def partner(me, step):
    other, bit = me, 1
    while bit <= step:
        if step & bit:
            other = other + bit * (1 - 2 * lax.rem(lax.div(me, bit), 2))
        bit *= 2
    return other


def alternate(peers):
    far, near = list(range(peers // 2, peers)), list(range(1, peers // 2))
    steps = []
    for i in range(peers // 2):
        steps += far[i : i + 1] + near[i : i + 1]
    return steps


def rotation(real, imag):
    return jnp.concatenate(
        [
            jnp.concatenate([real, imag], axis=1),
            jnp.concatenate([-imag, real], axis=1),
        ],
        axis=0,
    )


def fused_kernel(
    peers,
    sites,
    lower_hbm,
    diag_hbm,
    upper_hbm,
    sigma_hbm,
    coulomb_hbm,
    out_ref,
    greens,
    sigma_ref,
    coulomb_ref,
    halo,
    total,
    green_out,
    green_in,
    series,
    polar_out,
    polar_in,
    load_sem,
    coulomb_sem,
    halo_send,
    halo_recv,
    green_send,
    green_recv,
    polar_send,
    polar_recv,
):
    me = lax.axis_index("energy")
    site = lax.axis_index("space")
    has_next = site < sites - 1
    has_previous = site > 0
    next_site = lax.rem(site + 1, sites)
    previous_site = lax.rem(site + sites - 1, sites)
    local, order = greens.shape[0], greens.shape[-1]
    half = order // 2
    energies = peers * local
    steps = alternate(peers)
    f32, bf16 = jnp.float32, jnp.bfloat16

    barrier = pltpu.get_barrier_semaphore()
    for step in steps:
        pl.semaphore_signal(
            barrier, inc=1, device_id={"energy": partner(me, step)}, device_id_type=MESH
        )

    @pl.when(has_next)
    def _():
        pl.semaphore_signal(barrier, inc=1, device_id={"space": next_site}, device_id_type=MESH)

    @pl.when(has_previous)
    def _():
        pl.semaphore_signal(barrier, inc=1, device_id={"space": previous_site}, device_id_type=MESH)

    def load_sigma(energy):
        return pltpu.make_async_copy(
            sigma_hbm.at[:, 0, energy], sigma_ref.at[:, energy], load_sem.at[energy, 0]
        )

    sources = (diag_hbm, lower_hbm, upper_hbm)
    for energy in range(local):
        load_sigma(energy).start()
        for i, source in enumerate(sources):
            pltpu.make_async_copy(
                source.at[0, energy], greens.at[energy, i], load_sem.at[energy, 1]
            ).start()
    coulomb_load = pltpu.make_async_copy(coulomb_hbm.at[0], coulomb_ref, coulomb_sem)
    coulomb_load.start()

    neighbours = jnp.where(has_next, 1, 0) + jnp.where(has_previous, 1, 0)
    pl.semaphore_wait(barrier, peers - 1 + neighbours)

    def halo_copy(side, energy):
        return pltpu.make_async_remote_copy(
            src_ref=sigma_hbm.at[:, 0, energy],
            dst_ref=halo.at[side, energy],
            send_sem=halo_send.at[side, energy],
            recv_sem=halo_recv.at[side, energy],
            device_id={"space": next_site if side == 0 else previous_site},
            device_id_type=MESH,
        )

    def each_halo(energy, act):
        @pl.when(has_next)
        def _():
            act(halo_copy(0, energy))

        @pl.when(has_previous)
        def _():
            act(halo_copy(1, energy))

    for energy in range(local):
        each_halo(energy, lambda copy: copy.start())

    @pl.when(jnp.logical_not(has_previous))
    def _():
        halo[0] = jnp.zeros(halo.shape[1:], halo.dtype)

    @pl.when(jnp.logical_not(has_next))
    def _():
        halo[1] = jnp.zeros(halo.shape[1:], halo.dtype)

    early = max(local - 2, 0)

    def green_copy(other, slot, group, energies_sent, sides_sent):
        return pltpu.make_async_remote_copy(
            src_ref=green_out.at[other, energies_sent, sides_sent],
            dst_ref=green_in.at[slot, energies_sent, sides_sent],
            send_sem=green_send,
            recv_sem=green_recv.at[group, slot],
            device_id={"energy": other},
            device_id_type=MESH,
        )

    def send_green(group, first, count, side, sides):
        for step in steps:
            green_copy(
                partner(me, step), me, group, pl.ds(first, count), pl.ds(side, sides)
            ).start()

    def term(energy, terms):
        mixed, adjoint = [], []
        for which, sigma_of in terms:
            real, imag = greens[energy, which, 0], greens[energy, which, 1]
            wide = jnp.concatenate([real, imag], axis=1)
            mixed.append(
                jnp.concatenate(
                    [
                        jnp.dot(
                            wide,
                            rotation(sigma_of(kind, 0), sigma_of(kind, 1)),
                            preferred_element_type=f32,
                        ).astype(bf16)
                        for kind in range(2)
                    ],
                    axis=0,
                )
            )
            adjoint.append(
                jnp.concatenate(
                    [rotation(real[:half], imag[:half]), rotation(real[half:], imag[half:])],
                    axis=0,
                )
            )
        return lax.dot_general(
            jnp.concatenate(mixed, axis=1),
            jnp.concatenate(adjoint, axis=1),
            (((1,), (1,)), ((), ())),
            preferred_element_type=f32,
        )

    def own_term(energy):
        load_sigma(energy).wait()
        pltpu.make_async_copy(greens.at[energy], greens.at[energy], load_sem.at[energy, 1]).wait()
        total[energy] = term(energy, [(0, lambda kind, part: sigma_ref[kind, energy, part])])

    for energy in range(min(2, local)):
        own_term(energy)
    for energy in range(local):

        @pl.when(has_previous)
        def _():
            halo_copy(0, energy).wait_recv()

        @pl.when(has_next)
        def _():
            halo_copy(1, energy).wait_recv()

        coupled = term(
            energy,
            [
                (1, lambda kind, part: halo[0, energy, kind, part]),
                (2, lambda kind, part: halo[1, energy, kind, part]),
            ],
        )
        rounded = (total[energy] + coupled).astype(bf16)
        for side in range(2):
            for kind in range(2):
                block = rounded[
                    kind * order : (kind + 1) * order, side * order : (side + 1) * order
                ]
                green_out[:, energy, side, kind] = block.reshape(peers, ROWS, order)
        if energy < early:
            send_green(0, energy, 1, 0, 2)
        else:
            send_green(0, energy, 1, 0, 1)
        if energy == local - 1:
            send_green(1, early, local - early, 1, 1)
        if energy + 2 < local:
            own_term(energy + 2)

    coulomb_load.wait()
    coulomb = coulomb_ref[...]
    in_low = lax.broadcasted_iota(jnp.int32, (order, order), 1) < half
    straight = coulomb.astype(f32)
    swapped = pltpu.roll(straight, half, 1)
    zeros = jnp.zeros_like(straight)
    spread = jnp.concatenate(
        [
            jnp.concatenate(
                [jnp.where(in_low, straight, zeros), jnp.where(in_low, swapped, zeros)], axis=1
            ),
            jnp.concatenate(
                [jnp.where(in_low, zeros, swapped), jnp.where(in_low, zeros, straight)], axis=1
            ),
        ],
        axis=0,
    ).astype(bf16)

    fold = ROWS // 2
    low_lanes = lax.broadcasted_iota(jnp.int32, (local, fold, order), 2) < half

    def swap(values):
        return pltpu.roll(values.reshape(-1, order), half, 1).reshape(values.shape)

    tail = series.shape[3] - energies
    for side in range(2):
        for kind in range(2):
            for part in range(2):
                series[side, kind, part, energies:] = jnp.zeros((tail, fold, order), f32)

    def unpack(side, source, values):
        for kind in range(2):
            tile = values[:, kind].astype(f32)
            top, bottom = tile[:, :fold], tile[:, fold:]
            where = pl.ds(source * local, local)
            series[side, kind, 0, where] = jnp.where(low_lanes, top, swap(bottom))
            series[side, kind, 1, where] = jnp.where(low_lanes, swap(top), bottom)

    def units_of(ref, slot, units):
        if units % 2 == 0:
            return ref.at[slot, pl.ds(0, units // 2)]
        return ref.at[slot, pl.ds(0, units), 0]

    def receive_green(side):
        unpack(side, me, green_out[me, :, side])
        for step in steps:
            other = partner(me, step)
            units = 2 * early * (1 - side) + local - early
            arrived = units_of(green_in, other, units)
            pltpu.make_async_copy(arrived, arrived, green_recv.at[side, other]).wait()
            unpack(side, other, green_in[other, :, side])

    factor = 1.0 / math.sqrt(energies)

    def correlate(side, owner):
        first_lag = owner * local

        def some_energies(index, sums):
            start = index * local
            window = pl.ds(start + first_lag, 2 * local - 1)
            results = []
            for kind in range(2):
                sum_real, sum_imag = sums[2 * kind : 2 * kind + 2]
                ahead_real, ahead_imag = series[side, kind, 0, window], series[side, kind, 1, window]
                for i in range(local):
                    real = series[side, 1 - kind, 0, start + i]
                    imag = series[side, 1 - kind, 1, start + i]
                    shifted_real, shifted_imag = ahead_real[i : i + local], ahead_imag[i : i + local]
                    sum_real = sum_real + (shifted_real * real + shifted_imag * imag)
                    sum_imag = sum_imag + (shifted_imag * real - shifted_real * imag)
                results += [sum_real, sum_imag]
            return tuple(results)

        zero = jnp.zeros((local, fold, order), f32)
        sums = lax.fori_loop(0, peers - owner, some_energies, (zero,) * 4)
        tiles = []
        for kind in range(2):
            real, imag = sums[2 * kind] * factor, sums[2 * kind + 1] * factor
            top = jnp.where(low_lanes, real, swap(imag))
            bottom = jnp.where(low_lanes, swap(real), imag)
            tiles.append(jnp.concatenate([top, bottom], axis=1).astype(bf16))
        return tiles

    def polar_copy(other, slot, kind):
        where = (0,) if kind is None else (1, kind)
        return pltpu.make_async_remote_copy(
            src_ref=polar_out.at[where[0], other, *where[1:]],
            dst_ref=polar_in.at[where[0], slot, *where[1:]],
            send_sem=polar_send,
            recv_sem=polar_recv.at[0 if kind is None else 1 + kind],
            device_id={"energy": other},
            device_id_type=MESH,
        )

    for side in range(2):
        receive_green(side)
        for step in steps:
            other = partner(me, step)
            tiles = correlate(side, other)
            for kind in range(2):
                polar_out[side, other, kind] = tiles[kind]
            polar_copy(other, me, None if side == 0 else 0).start()
        if side == 1:
            for step in steps:
                polar_copy(partner(me, step), me, 1).start()
        tiles = correlate(side, me)
        for kind in range(2):
            polar_in[side, me, kind] = tiles[kind]

    for kind in range(2):
        if kind == 0:
            arrived = polar_in.at[0, pl.ds(0, peers - 1)]
            pltpu.make_async_copy(arrived, arrived, polar_recv.at[0]).wait()
        arrived = polar_in.at[1, pl.ds(0, peers - 1), kind]
        pltpu.make_async_copy(arrived, arrived, polar_recv.at[1 + kind]).wait()
        lefts = []
        for lag in range(local):
            both = jnp.concatenate(
                [polar_in[side, :, kind, lag].reshape(order, order) for side in range(2)], axis=1
            )
            lefts.append(jnp.dot(coulomb, both, preferred_element_type=f32).astype(bf16))
        screened = lax.dot_general(
            jnp.concatenate(lefts, axis=0),
            spread,
            (((1,), (1,)), ((), ())),
            preferred_element_type=f32,
        ).astype(bf16)
        for lag in range(local):
            rows = screened[lag * order : (lag + 1) * order]
            out_ref[kind, 0, lag, 0] = rows[:, :order]
            out_ref[kind, 0, lag, 1] = rows[:, order:]

    for energy in range(local):
        each_halo(energy, lambda copy: copy.wait_send())
    part = green_out.at[pl.ds(0, peers - 1)]
    pltpu.make_async_copy(part, part, green_send).wait()
    part = polar_out.at[:, pl.ds(0, peers - 1)]
    pltpu.make_async_copy(part, part, polar_send).wait()


def fused_body(green_lower, green_diag, green_upper, self_energy, coulomb):
    peers, sites = lax.axis_size("energy"), lax.axis_size("space")
    local, order = green_diag.shape[1], green_diag.shape[-1]
    bf16 = jnp.bfloat16
    share = (peers, local, 2, 2, ROWS, order)
    lags = (2, peers, 2, local, ROWS, order)
    series = (2, 2, 2, peers * local + local, ROWS // 2, order)
    dma = pltpu.SemaphoreType.DMA
    room = 64 * 2**20 - 2 * self_energy.size - 2**17
    return pl.pallas_call(
        functools.partial(fused_kernel, peers, sites),
        out_shape=pltpu.VMEM(self_energy.shape, bf16),
        in_specs=[pl.BlockSpec(memory_space=pltpu.HBM)] * 5,
        out_specs=pl.BlockSpec(memory_space=pltpu.VMEM),
        scratch_shapes=[
            pltpu.VMEM((local, 3, 2, order, order), bf16),
            pltpu.VMEM((2, local, 2, order, order), bf16),
            pltpu.VMEM((order, order), bf16),
            pltpu.VMEM((2, local, 2, 2, order, order), bf16),
            pltpu.VMEM((local, 2 * order, 2 * order), jnp.float32),
            pltpu.VMEM(share, bf16),
            pltpu.VMEM(share, bf16),
            pltpu.VMEM(series, jnp.float32),
            pltpu.VMEM(lags, bf16),
            pltpu.VMEM(lags, bf16),
            dma((local, 2)),
            dma,
            dma((2, local)),
            dma((2, local)),
            dma,
            dma((2, peers)),
            dma,
            dma((3,)),
        ],
        compiler_params=pltpu.CompilerParams(
            collective_id=0, has_side_effects=True, vmem_limit_bytes=room
        ),
    )(green_lower, green_diag, green_upper, self_energy, coulomb)


def body(green_lower, green_diag, green_upper, self_energy, coulomb):
    peers = lax.axis_size("energy")
    blocks, order = green_diag.shape[0], green_diag.shape[-1]
    if blocks == 1 and order == 128 and order == peers * ROWS and peers & (peers - 1) == 0:
        return fused_body(green_lower, green_diag, green_upper, self_energy, coulomb)
    return plain_body(green_lower, green_diag, green_upper, self_energy, coulomb)


def solution(mesh):
    in_specs = (
        P("space", "energy", None, None, None),
        P("space", "energy", None, None, None),
        P("space", "energy", None, None, None),
        P(None, "space", "energy", None, None, None),
        P("space", None, None),
    )
    out_specs = P(None, "space", "energy", None, None, None)
    return jax.shard_map(body, mesh=mesh, in_specs=in_specs, out_specs=out_specs, check_vma=False)
```

```python
import functools
import math

import jax
import jax.numpy as jnp
from jax import lax
from jax.experimental import pallas as pl
from jax.experimental.pallas import tpu as pltpu
from jax.sharding import PartitionSpec as P


def padded_2(shard, sides, width):
    for axis, dim in sides:
        peers, length = (lax.axis_size(axis), shard.shape[dim])
        up = [(i, (i + 1) % peers) for i in range(peers - 1)]
        down = [(j, i) for i, j in up]
        last = lax.slice_in_dim(shard, length - width, length, axis=dim)
        initial = lax.slice_in_dim(shard, 0, width, axis=dim)
        before = lax.ppermute(last, axis, up)
        after = lax.ppermute(initial, axis, down)
        shard = jnp.concatenate([before, shard, after], axis=dim)
    return shard


def congruence(green, sigma):
    green_real = green[:, :, 0]
    green_imag = green[:, :, 1]
    sigma_real = sigma[:, :, :, 0]
    sigma_imag = sigma[:, :, :, 1]
    green_wide = jnp.concatenate([green_real, green_imag], axis=-1)
    sigma_tall = jnp.concatenate(
        [
            jnp.concatenate([sigma_real, sigma_imag], axis=-1),
            jnp.concatenate([-sigma_imag, sigma_real], axis=-1),
        ],
        axis=-2,
    )
    mixed = jnp.einsum(
        "nepq,fneqr->fnepr", green_wide, sigma_tall, preferred_element_type=jnp.float32
    ).astype(jnp.bfloat16)
    adjoint_tall = jnp.concatenate(
        [green_wide, jnp.concatenate([-green_imag, green_real], axis=-1)], axis=-2
    )
    return jnp.einsum("fnepr,nesr->fneps", mixed, adjoint_tall, preferred_element_type=jnp.float32)


def split_table(table):
    high_part = table.astype(jnp.bfloat16)
    low_part = (table - high_part.astype(jnp.float32)).astype(jnp.bfloat16)
    return (high_part, low_part)


def spectrum(values, table_high, table_low, padded_len):

    def apply_table(part):
        return jnp.dot(table_high, part, preferred_element_type=jnp.float32) + jnp.dot(
            table_low, part, preferred_element_type=jnp.float32
        )

    real_terms = apply_table(values[:, 0])
    imag_terms = apply_table(values[:, 1])
    out_real = real_terms[:padded_len] + imag_terms[padded_len:]
    out_imag = imag_terms[:padded_len] - real_terms[padded_len:]
    return (out_real, out_imag)


def plain_body(green_lower, green_diag, green_upper, self_energy, coulomb):
    block_count = green_diag.shape[0]
    energy_local = green_diag.shape[1]
    block_order = green_diag.shape[-1]
    energies = energy_local * lax.axis_size("energy")
    padded_len = 2 * energies
    padded = padded_2(self_energy, (("space", 1),), 1)
    lower_term = congruence(green_lower, padded[:, :block_count])
    diag_term = congruence(green_diag, padded[:, 1 : block_count + 1])
    upper_term = congruence(green_upper, padded[:, 2:])
    total = lower_term + diag_term + upper_term
    total = total.reshape(2, block_count, energy_local, block_order, 2, block_order)
    green_function = (
        jnp.transpose(total, (0, 2, 4, 1, 3, 5))
        .astype(jnp.bfloat16)
        .reshape(2, energy_local, 2, -1)
    )
    frequency = lax.iota(jnp.int32, padded_len)
    energy_index = lax.iota(jnp.int32, energies)
    step_angle = 2.0 * math.pi / padded_len
    forward_angle = (frequency[:, None] * energy_index[None, :] % padded_len).astype(
        jnp.float32
    ) * step_angle
    forward_table = jnp.concatenate([jnp.cos(forward_angle), jnp.sin(forward_angle)], axis=0)
    table_high, table_low = split_table(forward_table)
    lesser_values = lax.all_to_all(
        green_function[0], "energy", split_axis=2, concat_axis=0, tiled=True
    )
    greater_values = lax.all_to_all(
        green_function[1], "energy", split_axis=2, concat_axis=0, tiled=True
    )
    lesser_real, lesser_imag = spectrum(lesser_values, table_high, table_low, padded_len)
    greater_real, greater_imag = spectrum(greater_values, table_high, table_low, padded_len)
    product_real = lesser_real * greater_real + lesser_imag * greater_imag
    product_imag = lesser_imag * greater_real - lesser_real * greater_imag
    row_index = jnp.concatenate([energy_index, (padded_len - energy_index) % padded_len])
    back_angle = (row_index[:, None] * frequency[None, :] % padded_len).astype(
        jnp.float32
    ) * step_angle
    back_cos = jnp.cos(back_angle)
    back_sin = jnp.sin(back_angle)
    back_table = jnp.concatenate(
        [
            jnp.concatenate([back_cos, -back_sin], axis=1),
            jnp.concatenate([back_sin, back_cos], axis=1),
        ],
        axis=0,
    )
    stacked_product = jnp.concatenate([product_real, product_imag], axis=0)
    factor = 1.0 / (padded_len * math.sqrt(energies))
    combined = (
        jnp.dot(
            back_table,
            stacked_product,
            precision=lax.Precision.HIGH,
            preferred_element_type=jnp.float32,
        )
        * factor
    )
    corr_real = combined[:padded_len]
    corr_imag = combined[padded_len:]
    lesser_lags = jnp.stack([corr_real[:energies], corr_imag[:energies]], axis=1)
    greater_lags = jnp.stack([corr_real[energies:], -corr_imag[energies:]], axis=1)
    polar = jnp.stack([lesser_lags, greater_lags], axis=0).astype(jnp.bfloat16)
    returned = lax.all_to_all(polar, "energy", split_axis=1, concat_axis=3, tiled=True)
    returned = returned.reshape(2, energy_local, 2, block_count, block_order, block_order)
    left_product = jnp.einsum(
        "npq,fetnqr->fetnpr", coulomb, returned, preferred_element_type=jnp.float32
    ).astype(jnp.bfloat16)
    screened = jnp.einsum(
        "fetnpr,nsr->fnetps", left_product, coulomb, preferred_element_type=jnp.float32
    )
    return screened.astype(jnp.bfloat16)


ROWS = 16
MESH = pl.DeviceIdType.MESH


def partner(me, step):
    other, bit = me, 1
    while bit <= step:
        if step & bit:
            other = other + bit * (1 - 2 * lax.rem(lax.div(me, bit), 2))
        bit *= 2
    return other


def far_first(peers):
    steps, span = [], peers // 2
    while span >= 1:
        steps += list(range(span, 2 * span))
        span //= 2
    return steps


def rotation(real, imag):
    return jnp.concatenate(
        [
            jnp.concatenate([real, imag], axis=1),
            jnp.concatenate([-imag, real], axis=1),
        ],
        axis=0,
    )


def fused_kernel(
    peers,
    sites,
    lower_hbm,
    diag_hbm,
    upper_hbm,
    sigma_hbm,
    coulomb_hbm,
    out_ref,
    greens,
    sigma_ref,
    coulomb_ref,
    halo,
    total,
    green_out,
    green_in,
    series,
    polar_out,
    polar_in,
    load_sem,
    coulomb_sem,
    halo_send,
    halo_recv,
    green_send,
    green_recv,
    polar_send,
    polar_recv,
):
    me = lax.axis_index("energy")
    site = lax.axis_index("space")
    has_next = site < sites - 1
    has_previous = site > 0
    next_site = lax.rem(site + 1, sites)
    previous_site = lax.rem(site + sites - 1, sites)
    local, order = greens.shape[0], greens.shape[-1]
    half = order // 2
    energies = peers * local
    steps = far_first(peers)
    f32, bf16 = jnp.float32, jnp.bfloat16

    barrier = pltpu.get_barrier_semaphore()
    for step in steps:
        pl.semaphore_signal(
            barrier, inc=1, device_id={"energy": partner(me, step)}, device_id_type=MESH
        )

    @pl.when(has_next)
    def _():
        pl.semaphore_signal(barrier, inc=1, device_id={"space": next_site}, device_id_type=MESH)

    @pl.when(has_previous)
    def _():
        pl.semaphore_signal(barrier, inc=1, device_id={"space": previous_site}, device_id_type=MESH)

    def load_sigma(energy):
        return pltpu.make_async_copy(
            sigma_hbm.at[:, 0, energy], sigma_ref.at[:, energy], load_sem.at[energy, 0]
        )

    sources = (diag_hbm, lower_hbm, upper_hbm)
    for energy in range(local):
        load_sigma(energy).start()
        for i, source in enumerate(sources):
            pltpu.make_async_copy(
                source.at[0, energy], greens.at[energy, i], load_sem.at[energy, 1]
            ).start()
    coulomb_load = pltpu.make_async_copy(coulomb_hbm.at[0], coulomb_ref, coulomb_sem)
    coulomb_load.start()

    neighbours = jnp.where(has_next, 1, 0) + jnp.where(has_previous, 1, 0)
    pl.semaphore_wait(barrier, peers - 1 + neighbours)

    def halo_copy(side, energy):
        return pltpu.make_async_remote_copy(
            src_ref=sigma_hbm.at[:, 0, energy],
            dst_ref=halo.at[side, energy],
            send_sem=halo_send.at[side, energy],
            recv_sem=halo_recv.at[side, energy],
            device_id={"space": next_site if side == 0 else previous_site},
            device_id_type=MESH,
        )

    def each_halo(energy, act):
        @pl.when(has_next)
        def _():
            act(halo_copy(0, energy))

        @pl.when(has_previous)
        def _():
            act(halo_copy(1, energy))

    for energy in range(local):
        each_halo(energy, lambda copy: copy.start())

    @pl.when(jnp.logical_not(has_previous))
    def _():
        halo[0] = jnp.zeros(halo.shape[1:], halo.dtype)

    @pl.when(jnp.logical_not(has_next))
    def _():
        halo[1] = jnp.zeros(halo.shape[1:], halo.dtype)

    early = max(local - 2, 0)

    def green_copy(other, slot, group, energies_sent, sides_sent):
        return pltpu.make_async_remote_copy(
            src_ref=green_out.at[other, energies_sent, sides_sent],
            dst_ref=green_in.at[slot, energies_sent, sides_sent],
            send_sem=green_send,
            recv_sem=green_recv.at[group, slot],
            device_id={"energy": other},
            device_id_type=MESH,
        )

    def send_green(group, first, count, side, sides):
        for step in steps:
            green_copy(
                partner(me, step), me, group, pl.ds(first, count), pl.ds(side, sides)
            ).start()

    def term(energy, terms):
        mixed, adjoint = [], []
        for which, sigma_of in terms:
            real, imag = greens[energy, which, 0], greens[energy, which, 1]
            wide = jnp.concatenate([real, imag], axis=1)
            mixed.append(
                jnp.concatenate(
                    [
                        jnp.dot(
                            wide,
                            rotation(sigma_of(kind, 0), sigma_of(kind, 1)),
                            preferred_element_type=f32,
                        ).astype(bf16)
                        for kind in range(2)
                    ],
                    axis=0,
                )
            )
            adjoint.append(
                jnp.concatenate(
                    [rotation(real[:half], imag[:half]), rotation(real[half:], imag[half:])],
                    axis=0,
                )
            )
        return lax.dot_general(
            jnp.concatenate(mixed, axis=1),
            jnp.concatenate(adjoint, axis=1),
            (((1,), (1,)), ((), ())),
            preferred_element_type=f32,
        )

    def own_term(energy):
        load_sigma(energy).wait()
        pltpu.make_async_copy(greens.at[energy], greens.at[energy], load_sem.at[energy, 1]).wait()
        total[energy] = term(energy, [(0, lambda kind, part: sigma_ref[kind, energy, part])])

    for energy in range(min(2, local)):
        own_term(energy)
    for energy in range(local):

        @pl.when(has_previous)
        def _():
            halo_copy(0, energy).wait_recv()

        @pl.when(has_next)
        def _():
            halo_copy(1, energy).wait_recv()

        coupled = term(
            energy,
            [
                (1, lambda kind, part: halo[0, energy, kind, part]),
                (2, lambda kind, part: halo[1, energy, kind, part]),
            ],
        )
        rounded = (total[energy] + coupled).astype(bf16)
        for side in range(2):
            for kind in range(2):
                block = rounded[
                    kind * order : (kind + 1) * order, side * order : (side + 1) * order
                ]
                green_out[:, energy, side, kind] = block.reshape(peers, ROWS, order)
        if energy < early:
            send_green(0, energy, 1, 0, 2)
        else:
            send_green(0, energy, 1, 0, 1)
        if energy == local - 1:
            send_green(1, early, local - early, 1, 1)
        if energy + 2 < local:
            own_term(energy + 2)

    coulomb_load.wait()
    coulomb = coulomb_ref[...]
    in_low = lax.broadcasted_iota(jnp.int32, (order, order), 1) < half
    straight = coulomb.astype(f32)
    swapped = pltpu.roll(straight, half, 1)
    zeros = jnp.zeros_like(straight)
    spread = jnp.concatenate(
        [
            jnp.concatenate(
                [jnp.where(in_low, straight, zeros), jnp.where(in_low, swapped, zeros)], axis=1
            ),
            jnp.concatenate(
                [jnp.where(in_low, zeros, swapped), jnp.where(in_low, zeros, straight)], axis=1
            ),
        ],
        axis=0,
    ).astype(bf16)

    fold = ROWS // 2
    low_lanes = lax.broadcasted_iota(jnp.int32, (local, fold, order), 2) < half

    def swap(values):
        return pltpu.roll(values.reshape(-1, order), half, 1).reshape(values.shape)

    tail = series.shape[3] - energies
    for side in range(2):
        for kind in range(2):
            for part in range(2):
                series[side, kind, part, energies:] = jnp.zeros((tail, fold, order), f32)

    def unpack(side, source, values):
        for kind in range(2):
            tile = values[:, kind].astype(f32)
            top, bottom = tile[:, :fold], tile[:, fold:]
            where = pl.ds(source * local, local)
            series[side, kind, 0, where] = jnp.where(low_lanes, top, swap(bottom))
            series[side, kind, 1, where] = jnp.where(low_lanes, swap(top), bottom)

    def units_of(ref, slot, units):
        if units % 2 == 0:
            return ref.at[slot, pl.ds(0, units // 2)]
        return ref.at[slot, pl.ds(0, units), 0]

    def receive_green(side):
        unpack(side, me, green_out[me, :, side])
        for step in steps:
            other = partner(me, step)
            units = 2 * early * (1 - side) + local - early
            arrived = units_of(green_in, other, units)
            pltpu.make_async_copy(arrived, arrived, green_recv.at[side, other]).wait()
            unpack(side, other, green_in[other, :, side])

    factor = 1.0 / math.sqrt(energies)

    def correlate(side, owner):
        first_lag = owner * local

        def some_energies(index, sums):
            start = index * local
            window = pl.ds(start + first_lag, 2 * local - 1)
            results = []
            for kind in range(2):
                sum_real, sum_imag = sums[2 * kind : 2 * kind + 2]
                ahead_real, ahead_imag = series[side, kind, 0, window], series[side, kind, 1, window]
                for i in range(local):
                    real = series[side, 1 - kind, 0, start + i]
                    imag = series[side, 1 - kind, 1, start + i]
                    shifted_real, shifted_imag = ahead_real[i : i + local], ahead_imag[i : i + local]
                    sum_real = sum_real + (shifted_real * real + shifted_imag * imag)
                    sum_imag = sum_imag + (shifted_imag * real - shifted_real * imag)
                results += [sum_real, sum_imag]
            return tuple(results)

        zero = jnp.zeros((local, fold, order), f32)
        sums = lax.fori_loop(0, peers - owner, some_energies, (zero,) * 4)
        tiles = []
        for kind in range(2):
            real, imag = sums[2 * kind] * factor, sums[2 * kind + 1] * factor
            top = jnp.where(low_lanes, real, swap(imag))
            bottom = jnp.where(low_lanes, swap(real), imag)
            tiles.append(jnp.concatenate([top, bottom], axis=1).astype(bf16))
        return tiles

    def polar_copy(other, slot, kind):
        where = (0,) if kind is None else (1, kind)
        return pltpu.make_async_remote_copy(
            src_ref=polar_out.at[where[0], other, *where[1:]],
            dst_ref=polar_in.at[where[0], slot, *where[1:]],
            send_sem=polar_send,
            recv_sem=polar_recv.at[0 if kind is None else 1 + kind],
            device_id={"energy": other},
            device_id_type=MESH,
        )

    for side in range(2):
        receive_green(side)
        for step in steps:
            other = partner(me, step)
            tiles = correlate(side, other)
            for kind in range(2):
                polar_out[side, other, kind] = tiles[kind]
            polar_copy(other, me, None if side == 0 else 0).start()
        if side == 1:
            for step in steps:
                polar_copy(partner(me, step), me, 1).start()
        tiles = correlate(side, me)
        for kind in range(2):
            polar_in[side, me, kind] = tiles[kind]

    for kind in range(2):
        if kind == 0:
            arrived = polar_in.at[0, pl.ds(0, peers - 1)]
            pltpu.make_async_copy(arrived, arrived, polar_recv.at[0]).wait()
        arrived = polar_in.at[1, pl.ds(0, peers - 1), kind]
        pltpu.make_async_copy(arrived, arrived, polar_recv.at[1 + kind]).wait()
        lefts = []
        for lag in range(local):
            both = jnp.concatenate(
                [polar_in[side, :, kind, lag].reshape(order, order) for side in range(2)], axis=1
            )
            lefts.append(jnp.dot(coulomb, both, preferred_element_type=f32).astype(bf16))
        screened = lax.dot_general(
            jnp.concatenate(lefts, axis=0),
            spread,
            (((1,), (1,)), ((), ())),
            preferred_element_type=f32,
        ).astype(bf16)
        for lag in range(local):
            rows = screened[lag * order : (lag + 1) * order]
            out_ref[kind, 0, lag, 0] = rows[:, :order]
            out_ref[kind, 0, lag, 1] = rows[:, order:]

    for energy in range(local):
        each_halo(energy, lambda copy: copy.wait_send())
    part = green_out.at[pl.ds(0, peers - 1)]
    pltpu.make_async_copy(part, part, green_send).wait()
    part = polar_out.at[:, pl.ds(0, peers - 1)]
    pltpu.make_async_copy(part, part, polar_send).wait()


def fused_body(green_lower, green_diag, green_upper, self_energy, coulomb):
    peers, sites = lax.axis_size("energy"), lax.axis_size("space")
    local, order = green_diag.shape[1], green_diag.shape[-1]
    bf16 = jnp.bfloat16
    share = (peers, local, 2, 2, ROWS, order)
    lags = (2, peers, 2, local, ROWS, order)
    series = (2, 2, 2, peers * local + local, ROWS // 2, order)
    dma = pltpu.SemaphoreType.DMA
    room = 64 * 2**20 - 2 * self_energy.size - 2**17
    return pl.pallas_call(
        functools.partial(fused_kernel, peers, sites),
        out_shape=pltpu.VMEM(self_energy.shape, bf16),
        in_specs=[pl.BlockSpec(memory_space=pltpu.HBM)] * 5,
        out_specs=pl.BlockSpec(memory_space=pltpu.VMEM),
        scratch_shapes=[
            pltpu.VMEM((local, 3, 2, order, order), bf16),
            pltpu.VMEM((2, local, 2, order, order), bf16),
            pltpu.VMEM((order, order), bf16),
            pltpu.VMEM((2, local, 2, 2, order, order), bf16),
            pltpu.VMEM((local, 2 * order, 2 * order), jnp.float32),
            pltpu.VMEM(share, bf16),
            pltpu.VMEM(share, bf16),
            pltpu.VMEM(series, jnp.float32),
            pltpu.VMEM(lags, bf16),
            pltpu.VMEM(lags, bf16),
            dma((local, 2)),
            dma,
            dma((2, local)),
            dma((2, local)),
            dma,
            dma((2, peers)),
            dma,
            dma((3,)),
        ],
        compiler_params=pltpu.CompilerParams(
            collective_id=0, has_side_effects=True, vmem_limit_bytes=room
        ),
    )(green_lower, green_diag, green_upper, self_energy, coulomb)


def body(green_lower, green_diag, green_upper, self_energy, coulomb):
    peers = lax.axis_size("energy")
    blocks, order = green_diag.shape[0], green_diag.shape[-1]
    if blocks == 1 and order == 128 and order == peers * ROWS and peers & (peers - 1) == 0:
        return fused_body(green_lower, green_diag, green_upper, self_energy, coulomb)
    return plain_body(green_lower, green_diag, green_upper, self_energy, coulomb)


def solution(mesh):
    in_specs = (
        P("space", "energy", None, None, None),
        P("space", "energy", None, None, None),
        P("space", "energy", None, None, None),
        P(None, "space", "energy", None, None, None),
        P("space", None, None),
    )
    out_specs = P(None, "space", "energy", None, None, None)
    return jax.shard_map(body, mesh=mesh, in_specs=in_specs, out_specs=out_specs, check_vma=False)
```
